128 devices in a mesh: gx: 16 (over y, x), gy: 8 (over z, core).
Axes of the slice: x: 4, y: 4, z: 4, core: 2. Of those that a mesh axis runs over, the one named last changes fastest.
Arguments:
- right_block: bfloat16 [262144, 768], P(('gx', 'gy')), may hold values from -6 to 6
- point_order: int32 [16, 8, 2048], P('gx', 'gy'), may hold values from 0 to 2047, each once within a row
- leaf_dense: bfloat16 [262144, 2048], P(('gx', 'gy')), may hold values from -0.125 to 0.125
- basis_in: bfloat16 [262144, 256], P(('gx', 'gy')), may hold values from -0.125 to 0.125
- basis_out: bfloat16 [262144, 256], P(('gx', 'gy')), may hold values from -0.1875 to 0.1875
- leaf_couple: bfloat16 [16, 8, 4, 256, 256], P('gx', 'gy'), may hold values from -0.375 to 0.375
- coarse_couple: bfloat16 [16, 8, 4, 256, 256], P('gx', 'gy'), may hold values from -1 to 1, as said below
- top_coupling: bfloat16 [2048, 2048], replicated, may hold values from -0.125 to 0.125
Outputs:
- product: bfloat16 [262144, 768], P(('gx', 'gy'))
The draws below stay inside these ranges and needn't reach their ends.
Inputs may be any that keep to these rules, and one draw needn't show every extreme that they name: coarse_couple[i, j] is equal over each aligned 2 x 2 block of leaves.
All inputs are finite; a program needn't handle non-finite values.
Results may differ from the reference program's by a relative error of at most 0.013.
Values may be sent and summed in bfloat16 or wider, within the bound.
No kernel may reach another device: no remote copies, remote signals or barrier semaphores. Data moves between devices by JAX's collectives and lax.ppermute only.
A program may use at most 128 MiB of HBM per device.

```python
import jax
import jax.numpy as jnp
from jax import lax

LEAF = 2048
RANK = 256
NCOL = 768
TOPS = 8
POINTS = 262144
N_GX = 16
N_GY = 8


def draw_coarse_couple(key, part):
    key = jax.random.fold_in(key, 7)
    small = jax.random.normal(key, (N_GX // 2, N_GY // 2, 4, RANK, RANK), jnp.float32)
    scales = jnp.array([(4.0 * RANK) ** (-0.5), RANK ** (-0.5), RANK ** (-0.5), RANK ** (-0.5)], jnp.float32)
    small = jnp.clip(small * scales[None, None, :, None, None], -1.0, 1.0)
    spread = jnp.repeat(jnp.repeat(small, 2, axis=0), 2, axis=1)
    return spread.astype(jnp.bfloat16)


def shard_levels(rng, dims, shards, least, largest):
    def one(position, blocks):
        draws = jax.random.uniform(jax.random.fold_in(jax.random.fold_in(rng, 6), position), (blocks,), jnp.float32, least / len(shards), largest / len(shards))
        return jnp.repeat(jnp.exp(draws), dims[position] // blocks).reshape((-1,) + (1,) * (len(dims) - position - 1))

    loudness = one(*shards[0])
    for cut in shards[1:]:
        loudness = loudness * one(*cut)
    return loudness


def normal_values(key, dims, width, bound, split=(), kind=jnp.bfloat16):
    loudness = shard_levels(key, dims, split, -0.22, 0.18) if split else 1.0
    drawn = jax.random.normal(key, dims, jnp.float32) * width * loudness
    return jnp.minimum(jnp.maximum(drawn, -bound), bound).astype(kind)


def setup_inputs(seed: int = 0) -> dict:
    arg_keys = jax.random.split(jax.random.key(seed), 9)
    return {
        "right_block": normal_values(arg_keys[0], (POINTS, NCOL), 1.0, 6.0, ((0, 128),)),
        "point_order": jax.vmap(lambda own: jax.random.permutation(own, LEAF))(jax.random.split(arg_keys[1], N_GX * N_GY)).reshape((N_GX, N_GY, LEAF)).astype(jnp.int32),
        "leaf_dense": normal_values(arg_keys[2], (POINTS, LEAF), LEAF ** -0.5, 0.125, ((0, 128),)),
        "basis_in": normal_values(arg_keys[3], (POINTS, RANK), LEAF ** -0.5, 0.125, ((0, 128),)),
        "basis_out": normal_values(arg_keys[4], (POINTS, RANK), (4 * RANK) ** -0.5, 0.1875, ((0, 128),)),
        "leaf_couple": normal_values(arg_keys[5], (N_GX, N_GY, 4, RANK, RANK), RANK ** -0.5, 0.375, ((0, 16), (1, 8))),
        "coarse_couple": draw_coarse_couple(jax.random.fold_in(arg_keys[8], 71), 0),
        "top_coupling": normal_values(arg_keys[7], (TOPS * RANK, TOPS * RANK), (TOPS * RANK) ** -0.5, 0.125),
    }


def flip_axis(values, along_dim, height):
    sizes_now = values.shape
    stride = 2 ** height
    if along_dim == 0:
        folded = values.reshape((sizes_now[0] // (2 * stride), 2, stride) + sizes_now[1:])
        folded = jnp.flip(folded, 1)
    else:
        folded = values.reshape((sizes_now[0], sizes_now[1] // (2 * stride), 2, stride) + sizes_now[2:])
        folded = jnp.flip(folded, 2)
    return folded.reshape(sizes_now)


def reference(right_block, point_order, leaf_dense, basis_in, basis_out, leaf_couple, coarse_couple, top_coupling):
    leaf_count = N_GX * N_GY
    block_grid = right_block.reshape(leaf_count, LEAF, NCOL)
    order_flat = point_order.reshape(leaf_count, LEAF).astype(jnp.int32)
    ordered = jax.vmap(lambda rows_in, order_row: jnp.take(rows_in, order_row, axis=0))(block_grid, order_flat)
    basis_grid = basis_in.reshape(leaf_count, LEAF, RANK)

    def leaf_coef(pieces):
        return jnp.dot(pieces[0].T, pieces[1], preferred_element_type=jnp.float32).astype(jnp.bfloat16)

    coefficient = lax.map(leaf_coef, (basis_grid, ordered)).reshape(N_GX, N_GY, RANK, NCOL)
    factors = [leaf_couple, coarse_couple]
    near_terms = []
    for height in range(2):
        mats = factors[height].astype(jnp.float32)
        coef_f = coefficient.astype(jnp.float32)
        lifted = jnp.einsum("xyrs,xyrn->xysn", mats[:, :, 0], coef_f).astype(jnp.bfloat16)
        side_x = flip_axis(coef_f, 0, height)
        side_y = flip_axis(coef_f, 1, height)
        side_xy = flip_axis(side_x, 1, height)
        near_sum = jnp.einsum("xyrs,xysn->xyrn", mats[:, :, 1], side_x)
        near_sum = near_sum + jnp.einsum("xyrs,xysn->xyrn", mats[:, :, 2], side_y)
        near_sum = near_sum + jnp.einsum("xyrs,xysn->xyrn", mats[:, :, 3], side_xy)
        near_terms.append(near_sum)
        pair_sum = (lifted.astype(jnp.float32) + flip_axis(lifted, 0, height).astype(jnp.float32)).astype(jnp.bfloat16)
        coefficient = (pair_sum.astype(jnp.float32) + flip_axis(pair_sum, 1, height).astype(jnp.float32)).astype(jnp.bfloat16)
    tops_x = N_GX // 4
    tops_y = N_GY // 4
    top_flat = coefficient[::4, ::4].reshape(TOPS * RANK, NCOL)
    box_of = jnp.arange(TOPS * RANK, dtype=jnp.int32) // RANK
    masked_top = jnp.where(box_of[:, None] == box_of[None, :], jnp.zeros((), jnp.bfloat16), top_coupling)
    downward = jnp.dot(masked_top, top_flat, preferred_element_type=jnp.float32).astype(jnp.bfloat16)
    downward = downward.reshape(tops_x, tops_y, RANK, NCOL)
    downward = jnp.repeat(jnp.repeat(downward, 4, axis=0), 4, axis=1)
    for height in (1, 0):
        mats = factors[height].astype(jnp.float32)
        lowered = jnp.einsum("xyrs,xysn->xyrn", mats[:, :, 0], downward.astype(jnp.float32))
        downward = (near_terms[height] + lowered).astype(jnp.bfloat16)
    down_flat = downward.reshape(leaf_count, RANK, NCOL)

    def leaf_out(pieces):
        dense_block, rows_in, basis_rows, down_leaf, order_row = pieces
        result = jnp.dot(dense_block, rows_in, preferred_element_type=jnp.float32)
        result = result + jnp.dot(basis_rows, down_leaf, preferred_element_type=jnp.float32)
        result = result.astype(jnp.bfloat16)
        return jnp.zeros((LEAF, NCOL), jnp.bfloat16).at[order_row].set(result)

    outputs = lax.map(leaf_out, (leaf_dense.reshape(leaf_count, LEAF, LEAF), ordered,
                                 basis_out.reshape(leaf_count, LEAF, RANK), down_flat, order_flat))
    return outputs.reshape(POINTS, NCOL)
```

```python
import functools

import jax
import jax.numpy as jnp
from jax import lax
from jax.experimental import pallas as pl
from jax.experimental.pallas import tpu as pltpu
from jax.sharding import PartitionSpec as P

AXES = ("gx", "gy")
F32 = jnp.float32
BF16 = jnp.bfloat16
LEAF = 2048
RANK = 256
NCOL = 768
HALF = NCOL // 2
QUARTER = NCOL // 4
VMEM = pl.BlockSpec(memory_space=pltpu.VMEM)
SMEM = pl.BlockSpec(memory_space=pltpu.SMEM)
ANY = pl.BlockSpec(memory_space=pl.ANY)
MIB = 1 << 20


def permute(array, dx=0, dy=0, turn=0):
    pairs = []
    for gx in range(16):
        for gy in range(8):
            to = ((gx + 4 * turn) % 16) ^ dx
            pairs.append((gx * 8 + gy, to * 8 + (gy ^ dy)))
    return lax.ppermute(array, AXES, pairs)


def nn(a, b):
    return jnp.dot(a, b, preferred_element_type=F32)


def nt(a, b):
    return lax.dot_general(a, b, (((1,), (1,)), ((), ())), preferred_element_type=F32)


def call(kernel, name, outs, in_specs, flops=0, moved=0, scratch=(), limit=16, aliases=None, grid=None, out_specs=None):
    shapes = [jax.ShapeDtypeStruct(*o) for o in outs]
    extra = {} if grid is None else {"grid": grid}
    return pl.pallas_call(
        kernel,
        out_shape=shapes,
        in_specs=in_specs,
        out_specs=[VMEM] * len(outs) if out_specs is None else out_specs,
        scratch_shapes=list(scratch),
        input_output_aliases=aliases or {},
        compiler_params=pltpu.CompilerParams(vmem_limit_bytes=limit * MIB),
        cost_estimate=pl.CostEstimate(flops=flops, bytes_accessed=moved, transcendentals=0),
        name=name,
        **extra,
    )


def picks(order_row, base, rows):
    it = lax.broadcasted_iota(jnp.int32, (rows, LEAF), 0)
    return jnp.where(it == (order_row - base), 1.0, 0.0).astype(BF16)


def front_kernel(pos, order, basis, x_hbm, couple, c0, send, keep, turned, x, lift, sem):
    fetch = pltpu.make_async_copy(x_hbm, x, sem)
    fetch.start()
    for j in range(LEAF // 512):
        block = nn(picks(order[...], j * 512, 512), basis[...]).astype(BF16)
        turned[:, j * 512 : (j + 1) * 512] = block.T
    fetch.wait()
    c = nn(turned[...], x[...]).astype(BF16).T
    c0[...] = c
    lift[...] = nn(c, couple[0]).astype(BF16)
    core = pos[0]
    keep[...] = lift[pl.ds(pl.multiple_of(core * HALF, HALF), HALF), :]
    send[...] = lift[pl.ds(pl.multiple_of((1 - core) * HALF, HALF), HALF), :]


def pair_kernel(pos, keep, recv, send2, keep2, total):
    total[...] = (keep[...].astype(F32) + recv[...].astype(F32)).astype(BF16)
    part = pos[1]
    keep2[...] = total[pl.ds(pl.multiple_of(part * QUARTER, QUARTER), QUARTER), :]
    send2[...] = total[pl.ds(pl.multiple_of((1 - part) * QUARTER, QUARTER), QUARTER), :]


def coarse_kernel(keep, recv, couple, _c0, _order, coef1, lift1, _c0_out):
    c = (keep[...].astype(F32) + recv[...].astype(F32)).astype(BF16)
    coef1[...] = c
    lift1[...] = nn(c, couple[0]).astype(BF16)


def sum_x_kernel(lift1, recv, coef1, _order, pair, coef1_out):
    pair[...] = (lift1[...].astype(F32) + recv[...].astype(F32)).astype(BF16)
    coef1_out[...] = coef1[...]


def sum_z_kernel(pair, recv, coef1, side_x, _order, coef2, both):
    coef2[...] = (pair[...].astype(F32) + recv[...].astype(F32)).astype(BF16)
    both[:QUARTER] = coef1[...]
    both[QUARTER:] = side_x[...]


def pick_top_kernel(pos, top, _order, rows, sems):
    y, z = pos[2], pos[3]
    copies = []
    for d in range(4):
        there = lax.rem(y + d, 4)
        r = pl.multiple_of((there * 2 + z) * RANK, RANK)
        s = pl.multiple_of(y * 2 * RANK, 2 * RANK)
        copies.append(
            pltpu.make_async_copy(top.at[pl.ds(r, RANK), pl.ds(s, 2 * RANK)], rows.at[d], sems.at[d])
        )
    for copy in copies:
        copy.start()
    for copy in copies:
        copy.wait()


def top_kernel(pos, own, other, rows, _order, q0, q1, q2, q3):
    low = pos[3] == 0
    a, b = own[...], other[...]
    zero = jnp.zeros_like(a)
    first = jnp.where(low, a, b)
    second = jnp.where(low, b, a)
    stay = jnp.concatenate([jnp.where(low, zero, b), jnp.where(low, b, zero)], axis=1)
    both = jnp.concatenate([first, second], axis=1)
    q0[...] = nt(stay, rows[0])
    q1[...] = nt(both, rows[1]).astype(BF16)
    q2[...] = nt(both, rows[2]).astype(BF16)
    q3[...] = nt(both, rows[3]).astype(BF16)


def near1_kernel(side_x, sides, couple, _order, near1):
    near1[...] = (
        nt(side_x[...], couple[1]) + nt(sides[:QUARTER], couple[2]) + nt(sides[QUARTER:], couple[3])
    )


def near0_kernel(side_x, side_y, side_xy, couple, _order, near0):
    near0[...] = nt(couple[1], side_x[...]) + nt(couple[2], side_y[...]) + nt(couple[3], side_xy[...])


def down1_kernel(q0, r1, r2, r3, near1, couple, _order, down1):
    d2 = (q0[...] + r1[...].astype(F32) + r2[...].astype(F32) + r3[...].astype(F32)).astype(BF16)
    down1[...] = (near1[...] + nt(d2, couple[0])).astype(BF16)


def gather_kernel(base, block, order, x, _order, out):
    start = base + pl.program_id(0) * block
    rows = []
    for s in range(block // 128):
        row = order[:, pl.ds(pl.multiple_of(start + s * 128, 128), 128)].astype(F32)
        column = jnp.broadcast_to(row, (128, 128)).T
        lane = lax.broadcasted_iota(jnp.int32, (128, 128), 1).astype(F32)
        rows.append(
            jnp.concatenate(
                [jnp.where(column == lane + 128.0 * j, 1.0, 0.0).astype(BF16) for j in range(LEAF // 128)], axis=1
            )
        )
    out[...] = nn(jnp.concatenate(rows, axis=0), x[...]).astype(BF16)


def dense_kernel(dense, upper, lower, _order, out):
    out[...] = (
        nn(dense[:, : LEAF // 2], upper[...]) + nn(dense[:, LEAF // 2 :], lower[...])
    ).astype(BF16)


def scatter_kernel(base, block, order, upper, lower, basis, _order, out, turned):
    hot = picks(order[...], base + pl.program_id(0) * block, block)
    out[...] = (nn(hot[:, : LEAF // 2], upper[...]) + nn(hot[:, LEAF // 2 :], lower[...])).astype(BF16)
    turned[...] = nn(hot, basis[...]).astype(BF16)


def final_kernel(pos, upper, lower, turned_u, turned_l, own, side, core_own, core_side, near0, couple, out, down1, down0):
    step = pl.program_id(0)

    @pl.when(step == 0)
    def _():
        core, part = pos[0], pos[1]
        for which, half, quarter in (
            (own, core, part),
            (side, core, 1 - part),
            (core_own, 1 - core, part),
            (core_side, 1 - core, 1 - part),
        ):
            down1[pl.ds(pl.multiple_of(half * HALF + quarter * QUARTER, QUARTER), QUARTER), :] = which[...]
        down0[...] = (near0[...] + nt(couple[0], down1[...])).astype(BF16)

    @pl.when(step < 4)
    def _():
        out[...] = (upper[...].astype(F32) + nn(turned_u[...], down0[...])).astype(BF16)

    @pl.when(step >= 4)
    def _():
        out[...] = (lower[...].astype(F32) + nn(turned_l[...], down0[...])).astype(BF16)


def fixed(shape):
    return pl.BlockSpec(shape, lambda i: (0,) * len(shape), pipeline_mode=pl.Buffered(1))


def gather_part(base, order, x, after):
    rows, block = LEAF // 2, 512
    return call(
        functools.partial(gather_kernel, base, block),
        "gather",
        [((rows, NCOL), BF16)],
        [fixed((1, LEAF)), fixed((LEAF, NCOL)), ANY],
        flops=2 * rows * LEAF * NCOL,
        moved=5 * MIB,
        limit=20,
        grid=(rows // block,),
        out_specs=[pl.BlockSpec((block, NCOL), lambda i: (i, 0))],
    )(order, x, after)[0]


def dense_part(part, dense, upper, lower, after):
    rows, block = LEAF // 2, 512
    steps = rows // block
    return call(
        dense_kernel,
        "dense",
        [((rows, NCOL), BF16)],
        [
            pl.BlockSpec((block, LEAF), lambda i: (part * steps + i, 0)),
            fixed((LEAF // 2, NCOL)),
            fixed((LEAF // 2, NCOL)),
            ANY,
        ],
        flops=2 * rows * LEAF * NCOL,
        moved=9 * MIB,
        limit=20,
        grid=(steps,),
        out_specs=[pl.BlockSpec((block, NCOL), lambda i: (i, 0))],
    )(dense, upper, lower, after)[0]


def scatter_part(base, order, upper, lower, basis, after):
    rows, block = LEAF // 2, 512
    return call(
        functools.partial(scatter_kernel, base, block),
        "scatter",
        [((rows, NCOL), BF16), ((rows, RANK), BF16)],
        [fixed((1, LEAF)), fixed((LEAF // 2, NCOL)), fixed((LEAF // 2, NCOL)), fixed((LEAF, RANK)), ANY],
        flops=2 * rows * LEAF * (NCOL + RANK),
        moved=7 * MIB,
        limit=20,
        grid=(rows // block,),
        out_specs=[pl.BlockSpec((block, NCOL), lambda i: (i, 0)), pl.BlockSpec((block, RANK), lambda i: (i, 0))],
    )(order, upper, lower, basis, after)


def local(right_block, point_order, leaf_dense, basis_in, basis_out, leaf_couple, coarse_couple, top_coupling):
    order = point_order.reshape(1, LEAF)
    leaf = leaf_couple.reshape(4, RANK, RANK)
    coarse = coarse_couple.reshape(4, RANK, RANK)
    gx = lax.axis_index("gx")
    gy = lax.axis_index("gy")
    pos = jnp.stack([gy % 2, (gx ^ (gx >> 1)) & 1, gx // 4, gy // 4]).astype(jnp.int32)
    quarter = ((QUARTER, RANK), BF16)
    half = ((HALF, RANK), BF16)
    whole = ((NCOL, RANK), BF16)
    small = 2 * QUARTER * RANK * RANK

    c0, send, keep = call(
        front_kernel,
        "front",
        [whole, half, half],
        [SMEM, VMEM, VMEM, ANY, VMEM],
        flops=2 * LEAF * LEAF * RANK + 2 * LEAF * RANK * NCOL,
        moved=5 * MIB,
        scratch=[
            pltpu.VMEM((RANK, LEAF), BF16),
            pltpu.VMEM((LEAF, NCOL), BF16),
            pltpu.VMEM((NCOL, RANK), BF16),
            pltpu.SemaphoreType.DMA,
        ],
        limit=24,
    )(pos, order, basis_in, right_block, leaf)
    recv = permute(send, dy=1)
    rows = call(
        pick_top_kernel,
        "pick_top",
        [((4, RANK, 2 * RANK), BF16)],
        [SMEM, ANY, ANY],
        moved=2 * MIB,
        scratch=[pltpu.SemaphoreType.DMA((4,))],
    )(pos, top_coupling, send)[0]

    send2, keep2 = call(
        pair_kernel, "pair", [quarter, quarter], [SMEM, VMEM, VMEM], scratch=[pltpu.VMEM((HALF, RANK), BF16)]
    )(pos, keep, recv)
    recv2 = permute(send2, dx=1)
    ordered_u = gather_part(0, order, right_block, send2)

    coef1, lift1, c0 = call(
        coarse_kernel,
        "coarse",
        [quarter, quarter, whole],
        [VMEM, VMEM, VMEM, ANY, ANY],
        flops=small,
        aliases={3: 2},
        out_specs=[VMEM, VMEM, ANY],
    )(keep2, recv2, coarse, c0, ordered_u)
    recv3 = permute(lift1, dx=3)
    side_y = permute(c0, dy=1)
    side_x = permute(c0, dx=1)
    side_xy = permute(side_x, dy=1)
    ordered_l = gather_part(LEAF // 2, order, right_block, lift1)

    pair, coef1 = call(sum_x_kernel, "sum_x", [quarter, quarter], [VMEM, VMEM, VMEM, ANY])(
        lift1, recv3, coef1, ordered_l
    )
    recv4 = permute(pair, dy=2)
    coarse_x = permute(coef1, dx=3)
    dense_u = dense_part(0, leaf_dense, ordered_u, ordered_l, pair)

    coef2, both = call(sum_z_kernel, "sum_z", [quarter, half], [VMEM, VMEM, VMEM, VMEM, ANY])(
        pair, recv4, coef1, coarse_x, dense_u
    )
    recv5 = permute(coef2, dy=6)
    coarse_yz = permute(both, dy=2)
    dense_l = dense_part(1, leaf_dense, ordered_u, ordered_l, coef2)

    q0, q1, q2, q3 = call(
        top_kernel,
        "top",
        [((QUARTER, RANK), F32), quarter, quarter, quarter],
        [SMEM, VMEM, VMEM, VMEM, ANY],
        flops=8 * small,
    )(pos, coef2, recv5, rows, dense_l)
    r2 = permute(q2, turn=2)
    r1 = permute(q1, turn=1)
    r3 = permute(q3, turn=3)
    out_u, turned_u = scatter_part(0, order, dense_u, dense_l, basis_out, q3)
    near1 = call(near1_kernel, "near1", [((QUARTER, RANK), F32)], [VMEM, VMEM, VMEM, ANY], flops=3 * small)(
        coarse_x, coarse_yz, coarse, q3
    )[0]

    down1 = call(down1_kernel, "down1", [quarter], [VMEM] * 6 + [ANY], flops=small)(
        q0, r1, r2, r3, near1, coarse, out_u
    )[0]
    side = permute(down1, dx=1)
    core_own = permute(down1, dy=1)
    core_side = permute(side, dy=1)
    out_l, turned_l = scatter_part(LEAF // 2, order, dense_u, dense_l, basis_out, down1)
    near0 = call(
        near0_kernel, "near0", [((RANK, NCOL), F32)], [VMEM] * 4 + [ANY], flops=12 * small
    )(side_x, side_y, side_xy, leaf, down1)[0]

    block = 256
    return call(
        final_kernel,
        "final",
        [((LEAF, NCOL), BF16)],
        [
            SMEM,
            pl.BlockSpec((block, NCOL), lambda i: (jnp.minimum(i, 3), 0)),
            pl.BlockSpec((block, NCOL), lambda i: (jnp.maximum(i - 4, 0), 0)),
            pl.BlockSpec((block, RANK), lambda i: (jnp.minimum(i, 3), 0)),
            pl.BlockSpec((block, RANK), lambda i: (jnp.maximum(i - 4, 0), 0)),
            fixed((QUARTER, RANK)),
            fixed((QUARTER, RANK)),
            fixed((QUARTER, RANK)),
            fixed((QUARTER, RANK)),
            fixed((RANK, NCOL)),
            fixed((1, RANK, RANK)),
        ],
        flops=2 * LEAF * RANK * NCOL,
        moved=8 * MIB,
        scratch=[pltpu.VMEM((NCOL, RANK), BF16), pltpu.VMEM((RANK, NCOL), BF16)],
        grid=(LEAF // block,),
        out_specs=[pl.BlockSpec((block, NCOL), lambda i: (i, 0))],
    )(pos, out_u, out_l, turned_u, turned_l, down1, side, core_own, core_side, near0, leaf)[0]


def solution(mesh):
    in_specs = (
        P(("gx", "gy"), None),
        P("gx", "gy", None),
        P(("gx", "gy"), None),
        P(("gx", "gy"), None),
        P(("gx", "gy"), None),
        P("gx", "gy", None, None, None),
        P("gx", "gy", None, None, None),
        P(),
    )
    out_specs = P(("gx", "gy"), None)
    return jax.shard_map(local, mesh=mesh, in_specs=in_specs, out_specs=out_specs, check_vma=False)
```

```python
import functools

import jax
import jax.numpy as jnp
from jax import lax
from jax.experimental import pallas as pl
from jax.experimental.pallas import tpu as pltpu
from jax.sharding import PartitionSpec as P

AXES = ("gx", "gy")
F32 = jnp.float32
BF16 = jnp.bfloat16
LEAF = 2048
RANK = 256
NCOL = 768
HALF = NCOL // 2
QUARTER = NCOL // 4
VMEM = pl.BlockSpec(memory_space=pltpu.VMEM)
HBM = pl.BlockSpec(memory_space=pltpu.HBM)
ANY = pl.BlockSpec(memory_space=pl.ANY)
MIB = 1 << 20


def permute(array, dx=0, dy=0):
    pairs = [(gx * 8 + gy, (gx ^ dx) * 8 + (gy ^ dy)) for gx in range(16) for gy in range(8)]
    return lax.ppermute(array, AXES, pairs)


def nn(a, b):
    return jnp.dot(a, b, preferred_element_type=F32)


def nt(a, b):
    return lax.dot_general(a, b, (((1,), (1,)), ((), ())), preferred_element_type=F32)


def add(a, b):
    return (a[...].astype(F32) + b[...].astype(F32)).astype(BF16)


def core_index():
    return lax.rem(lax.axis_index("gy"), 2)


def part_index():
    x = lax.rem(lax.axis_index("gx"), 4)
    return jnp.where((x == 1) | (x == 2), 1, 0)


def call(kernel, name, outs, in_specs, flops=0, moved=0, scratch=(), limit=16, aliases=None, out_specs=None):
    return pl.pallas_call(
        kernel,
        out_shape=[jax.ShapeDtypeStruct(*o) for o in outs],
        in_specs=in_specs,
        out_specs=[VMEM] * len(outs) if out_specs is None else out_specs,
        scratch_shapes=list(scratch),
        input_output_aliases=aliases or {},
        compiler_params=pltpu.CompilerParams(vmem_limit_bytes=limit * MIB),
        cost_estimate=pl.CostEstimate(flops=flops, bytes_accessed=moved, transcendentals=0),
        name=name,
    )


def picks(order_row, base, rows):
    it = lax.broadcasted_iota(jnp.int32, (rows, LEAF), 0)
    return jnp.where(it == (order_row - base), 1.0, 0.0).astype(BF16)


def front_kernel(order_hbm, basis_hbm, x_hbm, couple_hbm, c0, send, keep, order, basis, x, couple, turned, lift, sems):
    fetches = [
        pltpu.make_async_copy(order_hbm, order, sems.at[0]),
        pltpu.make_async_copy(basis_hbm, basis, sems.at[1]),
        pltpu.make_async_copy(couple_hbm.at[0], couple, sems.at[2]),
        pltpu.make_async_copy(x_hbm, x, sems.at[3]),
    ]
    for fetch in fetches:
        fetch.start()
    fetches[0].wait()
    fetches[1].wait()
    for j in range(LEAF // 512):
        block = nn(picks(order[...], j * 512, 512), basis[...]).astype(BF16)
        turned[:, j * 512 : (j + 1) * 512] = block.T
    fetches[3].wait()
    c = nn(turned[...], x[...]).astype(BF16).T
    c0[...] = c
    fetches[2].wait()
    lift[...] = nn(c, couple[...]).astype(BF16)
    core = core_index()
    keep[...] = lift[pl.ds(pl.multiple_of(core * HALF, HALF), HALF), :]
    send[...] = lift[pl.ds(pl.multiple_of((1 - core) * HALF, HALF), HALF), :]


def pair_kernel(keep, recv, _after, _ordered, send2, keep2, total):
    total[...] = add(keep, recv)
    part = part_index()
    keep2[...] = total[pl.ds(pl.multiple_of(part * QUARTER, QUARTER), QUARTER), :]
    send2[...] = total[pl.ds(pl.multiple_of((1 - part) * QUARTER, QUARTER), QUARTER), :]


def coarse_kernel(keep, recv, couple, _after, coef1, lift1):
    c = add(keep, recv)
    coef1[...] = c
    lift1[...] = nn(c, couple[0]).astype(BF16)


def sum_kernel(mine, recv, _after, total):
    total[...] = add(mine, recv)


def pick_top_kernel(top, _after, rows, sems):
    y = lax.axis_index("gx") // 4
    z = lax.axis_index("gy") // 4
    flip = jnp.where(lax.rem(y, 2) == 0, y + 1, y - 1)
    copies = []
    for d, there in enumerate((y, flip, 3 - y, 3 - flip)):
        r = pl.multiple_of((there * 2 + z) * RANK, RANK)
        s = pl.multiple_of(y * 2 * RANK, 2 * RANK)
        copies.append(
            pltpu.make_async_copy(top.at[pl.ds(r, RANK), pl.ds(s, 2 * RANK)], rows.at[d], sems.at[d])
        )
    for copy in copies:
        copy.start()
    for copy in copies:
        copy.wait()


def top_kernel(own, other, rows, _after, stay0, stay1, send):
    low = lax.axis_index("gy") < 4
    a, b = own[...], other[...]
    zero = jnp.zeros_like(a)
    both = jnp.concatenate([jnp.where(low, a, b), jnp.where(low, b, a)], axis=1)
    others = jnp.concatenate([jnp.where(low, zero, b), jnp.where(low, b, zero)], axis=1)
    send[:QUARTER] = nt(both, rows[2]).astype(BF16)
    send[QUARTER:] = nt(both, rows[3]).astype(BF16)
    stay0[...] = nt(others, rows[0])
    stay1[...] = nt(both, rows[1])


def half_kernel(stay1, recv, _after, send):
    send[...] = (stay1[...] + recv[QUARTER:].astype(F32)).astype(BF16)


def near1_kernel(side_x, sides, couple, _after, near1):
    near1[...] = (
        nt(side_x[...], couple[1]) + nt(sides[:QUARTER], couple[2]) + nt(sides[QUARTER:], couple[3])
    )


def near0_kernel(side_x, side_y, side_xy, couple, _after, near0):
    near0[...] = nt(couple[1], side_x[...]) + nt(couple[2], side_y[...]) + nt(couple[3], side_xy[...])


def down1_kernel(stay0, first, second, near1, couple, _after, _near0, down1):
    d2 = (stay0[...] + first[:QUARTER].astype(F32) + second[...].astype(F32)).astype(BF16)
    down1[...] = (near1[...] + nt(d2, couple[0])).astype(BF16)


def gather_kernel(blocks, first, order, x, _after, *refs):
    out = refs[first]
    for start, size in blocks:
        parts = []
        for s in range(start, start + size, 128):
            column = jnp.broadcast_to(order[:, s : s + 128].astype(F32), (128, 128)).T
            lane = lax.broadcasted_iota(jnp.int32, (128, 128), 1).astype(F32)
            parts.append(
                jnp.concatenate(
                    [jnp.where(column == lane + 128.0 * j, 1.0, 0.0).astype(BF16) for j in range(LEAF // 128)], axis=1
                )
            )
        out[start : start + size] = nn(jnp.concatenate(parts, axis=0), x[...]).astype(BF16)


def dense_kernel(blocks, first, dense, ordered, _after, *refs):
    out = refs[first]
    for start, size in blocks:
        out[start : start + size] = nn(dense[start : start + size], ordered[...]).astype(BF16)


def scatter_kernel(blocks, first, order, result, basis, _after, *refs):
    out, turned = refs[first : first + 2]
    for start, size in blocks:
        hot = picks(order[...], start, size)
        out[start : start + size] = nn(hot, result[...]).astype(BF16)
        turned[start : start + size] = nn(hot, basis[...]).astype(BF16)


def both_kernel(coef1, side_x, _after, both):
    both[:QUARTER] = coef1[...]
    both[QUARTER:] = side_x[...]


def gate_kernel(_array, _after, _out):
    pass


def final_kernel(base, turned, own, side, core_own, core_side, near0, couple, out_hbm, down1, out, sems):
    core, part = core_index(), part_index()
    for which, half, quarter in (
        (own, core, part),
        (side, core, 1 - part),
        (core_own, 1 - core, part),
        (core_side, 1 - core, 1 - part),
    ):
        down1[pl.ds(pl.multiple_of(half * HALF + quarter * QUARTER, QUARTER), QUARTER), :] = which[...]
    down0 = (near0[...] + nt(couple[0], down1[...])).astype(BF16)
    copies = []
    for j in range(4):
        rows = pl.ds(j * 512, 512)
        out[rows] = (base[rows].astype(F32) + nn(turned[rows], down0)).astype(BF16)
        copies.append(pltpu.make_async_copy(out.at[rows], out_hbm.at[rows], sems.at[j]))
        copies[-1].start()
    for copy in copies:
        copy.wait()


def leaf_part(kernel, name, blocks, operands, previous, widths, after, carry=()):
    outs = [((LEAF, width), BF16) for width in widths]
    kept = list(previous) + list(carry)
    count = len(operands) + 1
    skip = len(outs) - len(previous)
    got = call(
        functools.partial(kernel, blocks, len(kept)),
        name,
        outs + [(c.shape, c.dtype) for c in carry],
        [VMEM] * len(operands) + [ANY] + [VMEM] * len(previous) + [ANY] * len(carry),
        flops=2 * sum(size for _, size in blocks) * LEAF * sum(widths),
        moved=4 * MIB,
        aliases={count + i: skip + i for i in range(len(kept))},
        out_specs=[VMEM] * len(outs) + [ANY] * len(carry),
    )(*operands, after, *kept)
    return (got[: len(outs)], *got[len(outs) :])


def gate(array, after):
    return call(
        gate_kernel, "gate", [(array.shape, array.dtype)], [ANY, ANY], aliases={0: 0}, out_specs=[ANY]
    )(array, after)[0]


def local(right_block, point_order, leaf_dense, basis_in, basis_out, leaf_couple, coarse_couple, top_coupling):
    order = point_order.reshape(1, LEAF)
    leaf = leaf_couple.reshape(4, RANK, RANK)
    coarse = coarse_couple.reshape(4, RANK, RANK)
    quarter = ((QUARTER, RANK), BF16)
    quarter_f32 = ((QUARTER, RANK), F32)
    half = ((HALF, RANK), BF16)
    whole = ((NCOL, RANK), BF16)
    small = 2 * QUARTER * RANK * RANK

    c0, send, keep = call(
        front_kernel,
        "front",
        [whole, half, half],
        [HBM] * 4,
        flops=2 * LEAF * LEAF * RANK + 2 * LEAF * RANK * NCOL,
        moved=5 * MIB,
        scratch=[
            pltpu.VMEM((1, LEAF), jnp.int32),
            pltpu.VMEM((LEAF, RANK), BF16),
            pltpu.VMEM((LEAF, NCOL), BF16),
            pltpu.VMEM((RANK, RANK), BF16),
            pltpu.VMEM((RANK, LEAF), BF16),
            pltpu.VMEM((NCOL, RANK), BF16),
            pltpu.SemaphoreType.DMA((4,)),
        ],
        limit=24,
    )(*(pltpu.with_memory_space_constraint(a, pltpu.HBM) for a in (order, basis_in, right_block, leaf)))
    recv = permute(send, dy=1)
    rows = call(
        pick_top_kernel,
        "pick_top",
        [((4, RANK, 2 * RANK), BF16)],
        [HBM, ANY],
        moved=2 * MIB,
        scratch=[pltpu.SemaphoreType.DMA((4,))],
    )(pltpu.with_memory_space_constraint(top_coupling, pltpu.HBM), send)[0]

    gather = functools.partial(leaf_part, gather_kernel, "gather")
    dense = functools.partial(leaf_part, dense_kernel, "dense")
    scatter = functools.partial(leaf_part, scatter_kernel, "scatter")
    (ordered,) = gather([(0, 256)], [order, right_block], [], [NCOL], send)

    send2, keep2 = call(
        pair_kernel, "pair", [quarter, quarter], [VMEM, VMEM, ANY, ANY], scratch=[pltpu.VMEM((HALF, RANK), BF16)]
    )(keep, recv, rows, ordered[0])
    recv2 = permute(send2, dx=1)
    (ordered,) = gather([(256, 512), (768, 384)], [order, right_block], ordered, [NCOL], send2)

    coef1, lift1 = call(coarse_kernel, "coarse", [quarter, quarter], [VMEM, VMEM, VMEM, ANY], flops=small)(
        keep2, recv2, coarse, ordered[0]
    )
    recv3 = permute(lift1, dx=3)
    ordered, c0 = gather([(1152, 512), (1664, 384)], [order, right_block], ordered, [NCOL], lift1, [c0])
    side_y = permute(c0, dy=1)
    side_x = permute(c0, dx=1)

    pair = call(sum_kernel, "sum_x", [quarter], [VMEM, VMEM, ANY])(lift1, recv3, ordered[0])[0]
    recv4 = permute(pair, dy=2)
    result, coef1 = dense([(0, 512), (512, 512)], [leaf_dense, ordered[0]], [], [NCOL], pair, [coef1])
    coarse_x = permute(coef1, dx=3)

    coef2 = call(sum_kernel, "sum_z", [quarter], [VMEM, VMEM, ANY])(pair, recv4, result[0])[0]
    recv5 = permute(coef2, dy=6)
    (result,) = dense([(1024, 512), (1536, 512)], [leaf_dense, ordered[0]], result, [NCOL], coef2)
    both = call(both_kernel, "both", [half], [VMEM, VMEM, ANY])(coef1, coarse_x, result[0])[0]
    coarse_yz = permute(both, dy=2)

    stay0, stay1, send6 = call(
        top_kernel,
        "top",
        [quarter_f32, quarter_f32, half],
        [VMEM, VMEM, VMEM, ANY],
        flops=8 * small,
    )(coef2, recv5, rows, both)
    recv6 = permute(send6, dx=12)
    widths = [NCOL, RANK]
    scattered, side_x = scatter(
        [(0, 384), (384, 384)], [order, result[0], basis_out], [], widths, send6, [side_x]
    )
    side_xy = permute(side_x, dy=1)

    send7 = call(half_kernel, "half", [quarter], [VMEM, VMEM, ANY])(stay1, recv6, scattered[0])[0]
    recv7 = permute(send7, dx=4)
    near1 = call(near1_kernel, "near1", [quarter_f32], [VMEM, VMEM, VMEM, ANY], flops=3 * small)(
        coarse_x, coarse_yz, coarse, send7
    )[0]
    near0 = call(near0_kernel, "near0", [((RANK, NCOL), F32)], [VMEM] * 4 + [ANY], flops=12 * small)(
        side_x, side_y, side_xy, leaf, send7
    )[0]
    (scattered,) = scatter([(768, 320), (1088, 320)], [order, result[0], basis_out], scattered, widths, send7)

    down1 = call(down1_kernel, "down1", [quarter], [VMEM] * 5 + [ANY, ANY], flops=small)(
        stay0, recv6, recv7, near1, coarse, scattered[0], near0
    )[0]
    side = permute(down1, dx=1)
    core_own = permute(down1, dy=1)
    (scattered,) = scatter([(1408, 448)], [order, result[0], basis_out], scattered, widths, down1)
    side = gate(side, scattered[0])
    core_side = permute(side, dy=1)
    (scattered,) = scatter([(1856, 192)], [order, result[0], basis_out], scattered, widths, side)

    return call(
        final_kernel,
        "final",
        [((LEAF, NCOL), BF16)],
        [VMEM] * 8,
        flops=2 * LEAF * RANK * NCOL,
        moved=8 * MIB,
        scratch=[pltpu.VMEM((NCOL, RANK), BF16), pltpu.VMEM((LEAF, NCOL), BF16), pltpu.SemaphoreType.DMA((4,))],
        out_specs=[HBM],
    )(scattered[0], scattered[1], down1, side, core_own, core_side, near0, leaf)[0]


def solution(mesh):
    in_specs = (
        P(("gx", "gy"), None),
        P("gx", "gy", None),
        P(("gx", "gy"), None),
        P(("gx", "gy"), None),
        P(("gx", "gy"), None),
        P("gx", "gy", None, None, None),
        P("gx", "gy", None, None, None),
        P(),
    )
    out_specs = P(("gx", "gy"), None)
    return jax.shard_map(local, mesh=mesh, in_specs=in_specs, out_specs=out_specs, check_vma=False)
```

```python
import functools

import jax
import jax.numpy as jnp
from jax import lax
from jax.experimental import pallas as pl
from jax.experimental.pallas import tpu as pltpu
from jax.sharding import PartitionSpec as P

AXES = ("gx", "gy")
F32 = jnp.float32
BF16 = jnp.bfloat16
LEAF = 2048
RANK = 256
NCOL = 768
HALF = NCOL // 2
QUARTER = NCOL // 4
VMEM = pl.BlockSpec(memory_space=pltpu.VMEM)
HBM = pl.BlockSpec(memory_space=pltpu.HBM)
ANY = pl.BlockSpec(memory_space=pl.ANY)
MIB = 1 << 20


def permute(array, dx=0, dy=0):
    pairs = [(gx * 8 + gy, (gx ^ dx) * 8 + (gy ^ dy)) for gx in range(16) for gy in range(8)]
    return lax.ppermute(array, AXES, pairs)


def nn(a, b):
    return jnp.dot(a, b, preferred_element_type=F32)


def nt(a, b):
    return lax.dot_general(a, b, (((1,), (1,)), ((), ())), preferred_element_type=F32)


def add(a, b):
    return (a[...].astype(F32) + b[...].astype(F32)).astype(BF16)


def core_index():
    return lax.rem(lax.axis_index("gy"), 2)


def part_index():
    x = lax.rem(lax.axis_index("gx"), 4)
    return jnp.where((x == 1) | (x == 2), 1, 0)


def call(kernel, name, outs, in_specs, flops=0, moved=0, scratch=(), limit=16, aliases=None, out_specs=None):
    return pl.pallas_call(
        kernel,
        out_shape=[jax.ShapeDtypeStruct(*o) for o in outs],
        in_specs=in_specs,
        out_specs=[VMEM] * len(outs) if out_specs is None else out_specs,
        scratch_shapes=list(scratch),
        input_output_aliases=aliases or {},
        compiler_params=pltpu.CompilerParams(vmem_limit_bytes=limit * MIB),
        cost_estimate=pl.CostEstimate(flops=flops, bytes_accessed=moved, transcendentals=0),
        name=name,
    )


def picks(order_row, base, rows):
    it = lax.broadcasted_iota(jnp.int32, (rows, LEAF), 0)
    return jnp.where(it == (order_row - base), 1.0, 0.0).astype(BF16)


def front_kernel(
    order_hbm, basis_hbm, x_hbm, leaf_hbm, coarse_hbm, top,
    send, keep, c_both, x, order, rows, leaf, coarse,
    basis, turned, lift, sems,
):
    pairs = [(order_hbm, order), (basis_hbm, basis), (x_hbm, x), (leaf_hbm, leaf), (coarse_hbm, coarse)]
    y = lax.axis_index("gx") // 4
    z = lax.axis_index("gy") // 4
    flip = jnp.where(lax.rem(y, 2) == 0, y + 1, y - 1)
    for d, there in enumerate((y, flip, 3 - y, 3 - flip)):
        r = pl.multiple_of((there * 2 + z) * RANK, RANK)
        s = pl.multiple_of(y * 2 * RANK, 2 * RANK)
        pairs.append((top.at[pl.ds(r, RANK), pl.ds(s, 2 * RANK)], rows.at[d]))
    fetches = [pltpu.make_async_copy(here, there, sems.at[i]) for i, (here, there) in enumerate(pairs)]
    for fetch in fetches:
        fetch.start()
    fetches[0].wait()
    fetches[1].wait()
    flat = basis[...].T
    for j in range(LEAF // 512):
        turned[:, j * 512 : (j + 1) * 512] = nt(flat, picks(order[...], j * 512, 512)).astype(BF16)
    fetches[2].wait()
    c = nn(turned[...], x[...]).astype(BF16).T
    c_both[:NCOL] = c
    send[HALF:] = c
    fetches[3].wait()
    lift[...] = nn(c, leaf[0]).astype(BF16)
    core = core_index()
    keep[...] = lift[pl.ds(pl.multiple_of(core * HALF, HALF), HALF), :]
    send[:HALF] = lift[pl.ds(pl.multiple_of((1 - core) * HALF, HALF), HALF), :]
    for fetch in fetches[4:]:
        fetch.wait()


def pair_kernel(keep, recv, _after, _c_both, send2, keep2, c_both, total):
    total[...] = (keep[...].astype(F32) + recv[:HALF].astype(F32)).astype(BF16)
    part = part_index()
    keep2[...] = total[pl.ds(pl.multiple_of(part * QUARTER, QUARTER), QUARTER), :]
    send2[...] = total[pl.ds(pl.multiple_of((1 - part) * QUARTER, QUARTER), QUARTER), :]
    c_both[NCOL:] = recv[HALF:]


def coarse_kernel(keep, recv, couple, _after, coef1, lift1):
    c = add(keep, recv)
    coef1[...] = c
    lift1[...] = nn(c, couple[0]).astype(BF16)


def sum_kernel(mine, recv, _after, total):
    total[...] = add(mine, recv)


def both_tops(own, other, keep_own):
    low = lax.axis_index("gy") < 4
    b = other[...]
    a = own[...] if keep_own else jnp.zeros_like(b)
    return jnp.concatenate([jnp.where(low, a, b), jnp.where(low, b, a)], axis=1)


def top_send_kernel(own, other, rows, _after, send):
    both = both_tops(own, other, True)
    send[:QUARTER] = nt(both, rows[2]).astype(BF16)
    send[QUARTER:] = nt(both, rows[3]).astype(BF16)


def top_stay_kernel(own, other, rows, _after, stay0, stay1):
    stay0[...] = nt(both_tops(own, other, False), rows[0])
    stay1[...] = nt(both_tops(own, other, True), rows[1])


def half_kernel(stay1, recv, _after, send):
    send[...] = (stay1[...] + recv[QUARTER:].astype(F32)).astype(BF16)


def near1_kernel(side_x, sides, couple, _after, near1):
    near1[...] = (
        nt(side_x[...], couple[1]) + nt(sides[:QUARTER], couple[2]) + nt(sides[QUARTER:], couple[3])
    )


def near0_kernel(sides, recv, couple, _after, near0):
    near0[...] = nt(couple[1], sides[:NCOL]) + nt(couple[2], recv[HALF:]) + nt(couple[3], sides[NCOL:])


def down1_kernel(stay0, first, second, near1, couple, _after, down1):
    d2 = (stay0[...] + first[:QUARTER].astype(F32) + second[...].astype(F32)).astype(BF16)
    down1[...] = (near1[...] + nt(d2, couple[0])).astype(BF16)


def gather_kernel(blocks, first, order, x, _after, *refs):
    out = refs[first]
    for start, size in blocks:
        parts = []
        for s in range(start, start + size, 128):
            column = jnp.broadcast_to(order[:, s : s + 128].astype(F32), (128, 128)).T
            lane = lax.broadcasted_iota(jnp.int32, (128, 128), 1).astype(F32)
            parts.append(
                jnp.concatenate(
                    [jnp.where(column == lane + 128.0 * j, 1.0, 0.0).astype(BF16) for j in range(LEAF // 128)], axis=1
                )
            )
        out[start : start + size] = nn(jnp.concatenate(parts, axis=0), x[...]).astype(BF16)


def dense_kernel(blocks, first, dense, ordered, _after, *refs):
    out = refs[first]
    for start, size in blocks:
        out[start : start + size] = nn(dense[start : start + size], ordered[...]).astype(BF16)


def scatter_kernel(blocks, first, order, result, basis, _after, *refs):
    out, turned = refs[first : first + 2]
    for start, size in blocks:
        hot = picks(order[...], start, size)
        out[start : start + size] = nn(hot, result[...]).astype(BF16)
        turned[start : start + size] = nn(hot, basis[...]).astype(BF16)


def both_kernel(coef1, side_x, _after, both):
    both[:QUARTER] = coef1[...]
    both[QUARTER:] = side_x[...]


def join_kernel(own, side, _after, joined):
    part = part_index()
    joined[pl.ds(pl.multiple_of(part * QUARTER, QUARTER), QUARTER), :] = own[...]
    joined[pl.ds(pl.multiple_of((1 - part) * QUARTER, QUARTER), QUARTER), :] = side[...]


def leaf_half(base, turned, down1, near0, couple, cols, out, after_block):
    down0 = (near0[:, cols] + nt(couple[0], down1[...])).astype(BF16)
    for start, size in ((0, 512), (512, 512), (1024, 512), (1536, 256), (1792, 128), (1920, 128)):
        rows = pl.ds(start, size)
        out[rows] = (base[rows, cols].astype(F32) + nn(turned[rows], down0)).astype(BF16)
        after_block(rows)


def half_columns(own):
    core = core_index()
    return pl.ds(pl.multiple_of((core if own else 1 - core) * HALF, HALF), HALF)


def own_half_kernel(base, turned, down1, near0, couple, out_hbm, out, sems):
    cols = half_columns(True)
    copies = []

    def write(rows):
        if rows.start < LEAF // 2:
            copies.append(pltpu.make_async_copy(out.at[rows], out_hbm.at[rows, cols], sems.at[len(copies)]))
            copies[-1].start()

    leaf_half(base, turned, down1, near0, couple, cols, out, write)
    for copy in copies:
        copy.wait()


def final_kernel(base, turned, down1, near0, couple, own, _product, out_hbm, out, sems):
    lower = pl.ds(LEAF // 2, LEAF // 2)
    copies = [pltpu.make_async_copy(own.at[lower], out_hbm.at[lower, half_columns(True)], sems.at[0])]
    copies[0].start()
    cols = half_columns(False)

    def write(rows):
        copies.append(pltpu.make_async_copy(out.at[rows], out_hbm.at[rows, cols], sems.at[len(copies)]))
        copies[-1].start()

    leaf_half(base, turned, down1, near0, couple, cols, out, write)
    for copy in copies:
        copy.wait()


def leaf_part(kernel, name, blocks, operands, previous, widths, after, carry=()):
    outs = [((LEAF, width), BF16) for width in widths]
    kept = list(previous) + list(carry)
    count = len(operands) + 1
    skip = len(outs) - len(previous)
    got = call(
        functools.partial(kernel, blocks, len(kept)),
        name,
        outs + [(c.shape, c.dtype) for c in carry],
        [VMEM] * len(operands) + [ANY] + [VMEM] * len(previous) + [ANY] * len(carry),
        flops=2 * sum(size for _, size in blocks) * LEAF * sum(widths),
        moved=4 * MIB,
        aliases={count + i: skip + i for i in range(len(kept))},
        out_specs=[VMEM] * len(outs) + [ANY] * len(carry),
    )(*operands, after, *kept)
    return (got[: len(outs)], *got[len(outs) :])


def local(right_block, point_order, leaf_dense, basis_in, basis_out, leaf_couple, coarse_couple, top_coupling):
    couple = ((4, RANK, RANK), BF16)
    quarter = ((QUARTER, RANK), BF16)
    quarter_f32 = ((QUARTER, RANK), F32)
    half = ((HALF, RANK), BF16)
    small = 2 * QUARTER * RANK * RANK
    widths = [NCOL, RANK]
    gather = functools.partial(leaf_part, gather_kernel, "gather")
    dense = functools.partial(leaf_part, dense_kernel, "dense")
    scatter = functools.partial(leaf_part, scatter_kernel, "scatter")

    inputs = (
        point_order.reshape(1, LEAF),
        basis_in,
        right_block,
        leaf_couple.reshape(4, RANK, RANK),
        coarse_couple.reshape(4, RANK, RANK),
        top_coupling,
    )
    send, keep, c_both, x, order, rows, leaf, coarse = call(
        front_kernel,
        "front",
        [
            ((HALF + NCOL, RANK), BF16),
            half,
            ((2 * NCOL, RANK), BF16),
            ((LEAF, NCOL), BF16),
            ((1, LEAF), jnp.int32),
            ((4, RANK, 2 * RANK), BF16),
            couple,
            couple,
        ],
        [HBM] * 6,
        flops=2 * LEAF * LEAF * RANK + 2 * LEAF * RANK * NCOL,
        moved=7 * MIB,
        scratch=[
            pltpu.VMEM((LEAF, RANK), BF16),
            pltpu.VMEM((RANK, LEAF), BF16),
            pltpu.VMEM((NCOL, RANK), BF16),
            pltpu.SemaphoreType.DMA((9,)),
        ],
    )(*(pltpu.with_memory_space_constraint(a, pltpu.HBM) for a in inputs))
    recv = permute(send, dy=1)
    (ordered,) = gather([(0, 512)], [order, x], [], [NCOL], send)

    send2, keep2, c_both = call(
        pair_kernel,
        "pair",
        [quarter, quarter, ((2 * NCOL, RANK), BF16)],
        [VMEM, VMEM, ANY, VMEM],
        scratch=[pltpu.VMEM((HALF, RANK), BF16)],
        aliases={3: 2},
    )(keep, recv, ordered[0], c_both)
    recv2 = permute(send2, dx=1)
    (ordered,) = gather([(512, 640), (1152, 512)], [order, x], ordered, [NCOL], send2)

    coef1, lift1 = call(coarse_kernel, "coarse", [quarter, quarter], [VMEM, VMEM, VMEM, ANY], flops=small)(
        keep2, recv2, coarse, ordered[0]
    )
    recv3 = permute(lift1, dx=3)
    ordered, c_both = gather([(1664, 384)], [order, x], ordered, [NCOL], lift1, [c_both])
    sides = permute(c_both, dx=1)
    (result,) = dense([(0, 256)], [leaf_dense, ordered[0]], [], [NCOL], c_both)

    pair = call(sum_kernel, "sum_x", [quarter], [VMEM, VMEM, ANY])(lift1, recv3, result[0])[0]
    recv4 = permute(pair, dy=2)
    result, coef1 = dense([(256, 640)], [leaf_dense, ordered[0]], result, [NCOL], pair, [coef1])
    coarse_x = permute(coef1, dx=3)

    coef2 = call(sum_kernel, "sum_z", [quarter], [VMEM, VMEM, ANY])(pair, recv4, result[0])[0]
    recv5 = permute(coef2, dy=6)
    (result,) = dense([(896, 640)], [leaf_dense, ordered[0]], result, [NCOL], coef2)
    both = call(both_kernel, "both", [half], [VMEM, VMEM, ANY])(coef1, coarse_x, result[0])[0]
    coarse_yz = permute(both, dy=2)

    send6 = call(top_send_kernel, "top_send", [half], [VMEM, VMEM, VMEM, ANY], flops=4 * small)(
        coef2, recv5, rows, both
    )[0]
    recv6 = permute(send6, dx=12)
    stay0, stay1 = call(
        top_stay_kernel, "top_stay", [quarter_f32, quarter_f32], [VMEM, VMEM, VMEM, ANY], flops=4 * small
    )(coef2, recv5, rows, send6)
    (result,) = dense([(1536, 512)], [leaf_dense, ordered[0]], result, [NCOL], stay0)
    (scattered,) = scatter([(0, 640)], [order, result[0], basis_out], [], widths, stay0)

    send7 = call(half_kernel, "half", [quarter], [VMEM, VMEM, ANY])(stay1, recv6, scattered[0])[0]
    recv7 = permute(send7, dx=4)
    near1 = call(near1_kernel, "near1", [quarter_f32], [VMEM, VMEM, VMEM, ANY], flops=3 * small)(
        coarse_x, coarse_yz, coarse, send7
    )[0]
    (scattered,) = scatter([(640, 352), (992, 352)], [order, result[0], basis_out], scattered, widths, near1)

    down1 = call(down1_kernel, "down1", [quarter], [VMEM] * 5 + [ANY], flops=small)(
        stay0, recv6, recv7, near1, coarse, scattered[0]
    )[0]
    side = permute(down1, dx=1)
    near0 = call(near0_kernel, "near0", [((RANK, NCOL), F32)], [VMEM] * 3 + [ANY], flops=12 * small)(
        sides, recv, leaf, down1
    )[0]
    (scattered,) = scatter([(1344, 352), (1696, 352)], [order, result[0], basis_out], scattered, widths, near0)

    mine = call(join_kernel, "join", [half], [VMEM, VMEM, ANY])(down1, side, scattered[0])[0]
    other = permute(mine, dy=1)
    whole = ((LEAF, NCOL), BF16)
    product, own = call(
        own_half_kernel,
        "own_half",
        [whole, ((LEAF, HALF), BF16)],
        [VMEM] * 5,
        flops=LEAF * RANK * NCOL,
        moved=2 * MIB,
        scratch=[pltpu.SemaphoreType.DMA((2,))],
        out_specs=[HBM, VMEM],
    )(*scattered, mine, near0, leaf)
    return call(
        final_kernel,
        "final",
        [whole],
        [VMEM] * 6 + [HBM],
        flops=LEAF * RANK * NCOL,
        moved=4 * MIB,
        scratch=[pltpu.VMEM((LEAF, HALF), BF16), pltpu.SemaphoreType.DMA((7,))],
        out_specs=[HBM],
        aliases={6: 0},
    )(*scattered, other, near0, leaf, own, product)[0]


def solution(mesh):
    in_specs = (
        P(("gx", "gy"), None),
        P("gx", "gy", None),
        P(("gx", "gy"), None),
        P(("gx", "gy"), None),
        P(("gx", "gy"), None),
        P("gx", "gy", None, None, None),
        P("gx", "gy", None, None, None),
        P(),
    )
    out_specs = P(("gx", "gy"), None)
    return jax.shard_map(local, mesh=mesh, in_specs=in_specs, out_specs=out_specs, check_vma=False)
```

```python
import functools

import jax
import jax.numpy as jnp
from jax import lax
from jax.experimental import pallas as pl
from jax.experimental.pallas import tpu as pltpu
from jax.sharding import PartitionSpec as P

AXES = ("gx", "gy")
F32 = jnp.float32
BF16 = jnp.bfloat16
LEAF = 2048
RANK = 256
NCOL = 768
HALF = NCOL // 2
QUARTER = NCOL // 4
VMEM = pl.BlockSpec(memory_space=pltpu.VMEM)
HBM = pl.BlockSpec(memory_space=pltpu.HBM)
ANY = pl.BlockSpec(memory_space=pl.ANY)
MIB = 1 << 20


def permute(array, dx=0, dy=0):
    pairs = [(gx * 8 + gy, (gx ^ dx) * 8 + (gy ^ dy)) for gx in range(16) for gy in range(8)]
    return lax.ppermute(array, AXES, pairs)


def nn(a, b):
    return jnp.dot(a, b, preferred_element_type=F32)


def nt(a, b):
    return lax.dot_general(a, b, (((1,), (1,)), ((), ())), preferred_element_type=F32)


def add(a, b):
    return (a[...].astype(F32) + b[...].astype(F32)).astype(BF16)


def core_index():
    return lax.rem(lax.axis_index("gy"), 2)


def half_columns(own):
    core = core_index()
    return pl.ds(pl.multiple_of((core if own else 1 - core) * HALF, HALF), HALF)


def part_index():
    x = lax.rem(lax.axis_index("gx"), 4)
    return jnp.where((x == 1) | (x == 2), 1, 0)


def call(kernel, name, outs, in_specs, flops=0, moved=0, scratch=(), limit=16, aliases=None, out_specs=None):
    return pl.pallas_call(
        kernel,
        out_shape=[jax.ShapeDtypeStruct(*o) for o in outs],
        in_specs=in_specs,
        out_specs=[VMEM] * len(outs) if out_specs is None else out_specs,
        scratch_shapes=list(scratch),
        input_output_aliases=aliases or {},
        compiler_params=pltpu.CompilerParams(vmem_limit_bytes=limit * MIB),
        cost_estimate=pl.CostEstimate(flops=flops, bytes_accessed=moved, transcendentals=0),
        name=name,
    )


def picks(order_row, base, rows):
    it = lax.broadcasted_iota(jnp.int32, (rows, LEAF), 0)
    return jnp.where(it == (order_row - base), 1.0, 0.0).astype(BF16)


def front_kernel(
    order_hbm, basis_hbm, x_hbm, leaf_hbm, coarse_hbm, top,
    send, c_both, x, order, turned, rows, leaf, coarse,
    basis, sems,
):
    pairs = [(order_hbm, order), (basis_hbm, basis), (x_hbm, x), (leaf_hbm, leaf), (coarse_hbm, coarse)]
    y = lax.axis_index("gx") // 4
    z = lax.axis_index("gy") // 4
    flip = jnp.where(lax.rem(y, 2) == 0, y + 1, y - 1)
    for d, there in enumerate((y, flip, 3 - y, 3 - flip)):
        r = pl.multiple_of((there * 2 + z) * RANK, RANK)
        s = pl.multiple_of(y * 2 * RANK, 2 * RANK)
        pairs.append((top.at[pl.ds(r, RANK), pl.ds(s, 2 * RANK)], rows.at[d]))
    fetches = [pltpu.make_async_copy(here, there, sems.at[i]) for i, (here, there) in enumerate(pairs)]
    for fetch in fetches:
        fetch.start()
    fetches[0].wait()
    fetches[1].wait()
    flat = basis[...].T
    for j in range(LEAF // 512):
        turned[:, j * 512 : (j + 1) * 512] = nt(flat, picks(order[...], j * 512, 512)).astype(BF16)
    fetches[2].wait()
    fetches[3].wait()
    cols = half_columns(False)
    c = nn(turned[...], x[:, cols]).astype(BF16).T
    c_both[cols] = c
    send[...] = nn(c, leaf[0]).astype(BF16)
    for fetch in fetches[4:]:
        fetch.wait()


def own_coef_kernel(turned, x, leaf, _c_both, _after, keep, c_both, c_own):
    cols = half_columns(True)
    c = nn(turned[...], x[:, cols]).astype(BF16).T
    c_both[cols] = c
    keep[...] = nn(c, leaf[0]).astype(BF16)
    c_own[...] = c_both[:NCOL]


def pair_kernel(keep, recv, send2, keep2, total):
    total[...] = add(keep, recv)
    part = part_index()
    keep2[...] = total[pl.ds(pl.multiple_of(part * QUARTER, QUARTER), QUARTER), :]
    send2[...] = total[pl.ds(pl.multiple_of((1 - part) * QUARTER, QUARTER), QUARTER), :]


def fill_kernel(recv, _c_both, _after, c_both):
    c_both[NCOL:] = recv[...]


def coarse_kernel(keep, recv, couple, _after, coef1, lift1):
    c = add(keep, recv)
    coef1[...] = c
    lift1[...] = nn(c, couple[0]).astype(BF16)


def sum_kernel(mine, recv, _after, total):
    total[...] = add(mine, recv)


def both_tops(own, other, keep_own):
    low = lax.axis_index("gy") < 4
    b = other[...]
    a = own[...] if keep_own else jnp.zeros_like(b)
    return jnp.concatenate([jnp.where(low, a, b), jnp.where(low, b, a)], axis=1)


def top_send_kernel(own, other, rows, _after, send):
    both = both_tops(own, other, True)
    send[:QUARTER] = nt(both, rows[2]).astype(BF16)
    send[QUARTER:] = nt(both, rows[3]).astype(BF16)


def top_stay_kernel(own, other, rows, _after, stay0, stay1):
    stay0[...] = nt(both_tops(own, other, False), rows[0])
    stay1[...] = nt(both_tops(own, other, True), rows[1])


def half_kernel(stay1, recv, _after, send):
    send[...] = (stay1[...] + recv[QUARTER:].astype(F32)).astype(BF16)


def near1_kernel(side_x, sides, couple, _after, near1):
    near1[...] = (
        nt(side_x[...], couple[1]) + nt(sides[:QUARTER], couple[2]) + nt(sides[QUARTER:], couple[3])
    )


def near0_kernel(sides, recv, couple, _after, near0):
    near0[...] = nt(couple[1], sides[:NCOL]) + nt(couple[2], recv[...]) + nt(couple[3], sides[NCOL:])


def down1_kernel(stay0, first, second, near1, couple, _after, down1):
    d2 = (stay0[...] + first[:QUARTER].astype(F32) + second[...].astype(F32)).astype(BF16)
    down1[...] = (near1[...] + nt(d2, couple[0])).astype(BF16)


def gather_kernel(blocks, first, order, x, _after, *refs):
    out = refs[first]
    for start, size in blocks:
        parts = []
        for s in range(start, start + size, 128):
            column = jnp.broadcast_to(order[:, s : s + 128].astype(F32), (128, 128)).T
            lane = lax.broadcasted_iota(jnp.int32, (128, 128), 1).astype(F32)
            parts.append(
                jnp.concatenate(
                    [jnp.where(column == lane + 128.0 * j, 1.0, 0.0).astype(BF16) for j in range(LEAF // 128)], axis=1
                )
            )
        out[start : start + size] = nn(jnp.concatenate(parts, axis=0), x[...]).astype(BF16)


def dense_kernel(blocks, first, dense, ordered, _after, *refs):
    out = refs[first]
    for start, size in blocks:
        out[start : start + size] = nn(dense[start : start + size], ordered[...]).astype(BF16)


def scatter_kernel(blocks, first, order, result, basis, _after, *refs):
    out, turned = refs[first : first + 2]
    for start, size in blocks:
        hot = picks(order[...], start, size)
        out[start : start + size] = nn(hot, result[...]).astype(BF16)
        turned[start : start + size] = nn(hot, basis[...]).astype(BF16)


def both_kernel(coef1, side_x, _after, both):
    both[:QUARTER] = coef1[...]
    both[QUARTER:] = side_x[...]


def join_kernel(own, side, _after, joined):
    part = part_index()
    joined[pl.ds(pl.multiple_of(part * QUARTER, QUARTER), QUARTER), :] = own[...]
    joined[pl.ds(pl.multiple_of((1 - part) * QUARTER, QUARTER), QUARTER), :] = side[...]


def leaf_half(base, turned, down1, near0, couple, cols, out, after_block):
    down0 = (near0[:, cols] + nt(couple[0], down1[...])).astype(BF16)
    for start, size in ((0, 512), (512, 512), (1024, 512), (1536, 256), (1792, 128), (1920, 128)):
        rows = pl.ds(start, size)
        out[rows] = (base[rows, cols].astype(F32) + nn(turned[rows], down0)).astype(BF16)
        after_block(rows)


def own_half_kernel(which, base, turned, down1, near0, couple, *refs):
    out_hbm, out, sems = refs[-3 - (which == 1)], refs[-2 - (which == 1)], refs[-1]

    @pl.when(core_index() == which)
    def _():
        cols = half_columns(True)
        copies = []

        def write(rows):
            if rows.start < LEAF // 2:
                copies.append(pltpu.make_async_copy(out.at[rows], out_hbm.at[rows, cols], sems.at[len(copies)]))
                copies[-1].start()

        leaf_half(base, turned, down1, near0, couple, cols, out, write)
        for copy in copies:
            copy.wait()


def final_kernel(base, turned, down1, near0, couple, own, _product, out_hbm, out, sems):
    lower = pl.ds(LEAF // 2, LEAF // 2)
    copies = [pltpu.make_async_copy(own.at[lower], out_hbm.at[lower, half_columns(True)], sems.at[0])]
    copies[0].start()
    cols = half_columns(False)

    def write(rows):
        copies.append(pltpu.make_async_copy(out.at[rows], out_hbm.at[rows, cols], sems.at[len(copies)]))
        copies[-1].start()

    leaf_half(base, turned, down1, near0, couple, cols, out, write)
    for copy in copies:
        copy.wait()


def leaf_part(kernel, name, blocks, operands, previous, widths, after, carry=()):
    outs = [((LEAF, width), BF16) for width in widths]
    kept = list(previous) + list(carry)
    count = len(operands) + 1
    skip = len(outs) - len(previous)
    got = call(
        functools.partial(kernel, blocks, len(kept)),
        name,
        outs + [(c.shape, c.dtype) for c in carry],
        [VMEM] * len(operands) + [ANY] + [VMEM] * len(previous) + [ANY] * len(carry),
        flops=2 * sum(size for _, size in blocks) * LEAF * sum(widths),
        moved=4 * MIB,
        aliases={count + i: skip + i for i in range(len(kept))},
        out_specs=[VMEM] * len(outs) + [ANY] * len(carry),
    )(*operands, after, *kept)
    return (got[: len(outs)], *got[len(outs) :])


def local(right_block, point_order, leaf_dense, basis_in, basis_out, leaf_couple, coarse_couple, top_coupling):
    couple = ((4, RANK, RANK), BF16)
    quarter = ((QUARTER, RANK), BF16)
    quarter_f32 = ((QUARTER, RANK), F32)
    half = ((HALF, RANK), BF16)
    small = 2 * QUARTER * RANK * RANK
    widths = [NCOL, RANK]
    gather = functools.partial(leaf_part, gather_kernel, "gather")
    dense = functools.partial(leaf_part, dense_kernel, "dense")
    scatter = functools.partial(leaf_part, scatter_kernel, "scatter")

    inputs = (
        point_order.reshape(1, LEAF),
        basis_in,
        right_block,
        leaf_couple.reshape(4, RANK, RANK),
        coarse_couple.reshape(4, RANK, RANK),
        top_coupling,
    )
    both_coefs = ((2 * NCOL, RANK), BF16)
    send, c_both, x, order, turned_basis, rows, leaf, coarse = call(
        front_kernel,
        "front",
        [
            half,
            both_coefs,
            ((LEAF, NCOL), BF16),
            ((1, LEAF), jnp.int32),
            ((RANK, LEAF), BF16),
            ((4, RANK, 2 * RANK), BF16),
            couple,
            couple,
        ],
        [HBM] * 6,
        flops=2 * LEAF * LEAF * RANK + LEAF * RANK * NCOL,
        moved=7 * MIB,
        scratch=[pltpu.VMEM((LEAF, RANK), BF16), pltpu.SemaphoreType.DMA((9,))],
    )(*(pltpu.with_memory_space_constraint(a, pltpu.HBM) for a in inputs))
    recv = permute(send, dy=1)
    keep, c_both, c_own = call(
        own_coef_kernel,
        "own_coef",
        [half, both_coefs, ((NCOL, RANK), BF16)],
        [VMEM] * 4 + [ANY],
        flops=LEAF * RANK * NCOL,
        moved=2 * MIB,
        aliases={3: 1},
    )(turned_basis, x, leaf, c_both, send)
    c_core = permute(c_own, dy=1)

    send2, keep2 = call(
        pair_kernel, "pair", [quarter, quarter], [VMEM, VMEM], scratch=[pltpu.VMEM((HALF, RANK), BF16)]
    )(keep, recv)
    recv2 = permute(send2, dx=1)
    (ordered,) = gather([(0, 640), (640, 512)], [order, x], [], [NCOL], send2)

    coef1, lift1 = call(coarse_kernel, "coarse", [quarter, quarter], [VMEM, VMEM, VMEM, ANY], flops=small)(
        keep2, recv2, coarse, ordered[0]
    )
    recv3 = permute(lift1, dx=3)
    (ordered,) = gather([(1152, 512), (1664, 384)], [order, x], ordered, [NCOL], lift1)
    c_both = call(fill_kernel, "fill", [both_coefs], [VMEM, VMEM, ANY], aliases={1: 0})(
        c_core, c_both, ordered[0]
    )[0]
    sides = permute(c_both, dx=1)

    pair = call(sum_kernel, "sum_x", [quarter], [VMEM, VMEM, ANY])(lift1, recv3, c_both)[0]
    recv4 = permute(pair, dy=2)
    result, coef1 = dense([(0, 576)], [leaf_dense, ordered[0]], [], [NCOL], pair, [coef1])
    coarse_x = permute(coef1, dx=3)

    coef2 = call(sum_kernel, "sum_z", [quarter], [VMEM, VMEM, ANY])(pair, recv4, result[0])[0]
    recv5 = permute(coef2, dy=6)
    (result,) = dense([(576, 640)], [leaf_dense, ordered[0]], result, [NCOL], coef2)
    both = call(both_kernel, "both", [half], [VMEM, VMEM, ANY])(coef1, coarse_x, result[0])[0]
    coarse_yz = permute(both, dy=2)

    send6 = call(top_send_kernel, "top_send", [half], [VMEM, VMEM, VMEM, ANY], flops=4 * small)(
        coef2, recv5, rows, both
    )[0]
    recv6 = permute(send6, dx=12)
    stay0, stay1 = call(
        top_stay_kernel, "top_stay", [quarter_f32, quarter_f32], [VMEM, VMEM, VMEM, ANY], flops=4 * small
    )(coef2, recv5, rows, send6)
    (result,) = dense([(1216, 416), (1632, 416)], [leaf_dense, ordered[0]], result, [NCOL], stay0)
    (scattered,) = scatter([(0, 512)], [order, result[0], basis_out], [], widths, stay0)

    send7 = call(half_kernel, "half", [quarter], [VMEM, VMEM, ANY])(stay1, recv6, scattered[0])[0]
    recv7 = permute(send7, dx=4)
    near1 = call(near1_kernel, "near1", [quarter_f32], [VMEM, VMEM, VMEM, ANY], flops=3 * small)(
        coarse_x, coarse_yz, coarse, send7
    )[0]
    (scattered,) = scatter([(512, 768)], [order, result[0], basis_out], scattered, widths, near1)

    down1 = call(down1_kernel, "down1", [quarter], [VMEM] * 5 + [ANY], flops=small)(
        stay0, recv6, recv7, near1, coarse, scattered[0]
    )[0]
    side = permute(down1, dx=1)
    near0 = call(near0_kernel, "near0", [((RANK, NCOL), F32)], [VMEM] * 3 + [ANY], flops=12 * small)(
        sides, c_core, leaf, down1
    )[0]
    (scattered,) = scatter([(1280, 768)], [order, result[0], basis_out], scattered, widths, near0)

    mine = call(join_kernel, "join", [half], [VMEM, VMEM, ANY])(down1, side, scattered[0])[0]
    whole = ((LEAF, NCOL), BF16)
    halves = [whole, ((LEAF, HALF), BF16)]
    costs = dict(flops=LEAF * RANK * NCOL, moved=2 * MIB, scratch=[pltpu.SemaphoreType.DMA((2,))])
    product, own, mine = call(
        functools.partial(own_half_kernel, 1),
        "own_half_1",
        halves + [half],
        [VMEM] * 5,
        out_specs=[HBM, VMEM, VMEM],
        aliases={2: 2},
        **costs,
    )(*scattered, mine, near0, leaf)
    other = permute(mine, dy=1)
    product, own = call(
        functools.partial(own_half_kernel, 0),
        "own_half_0",
        halves,
        [VMEM] * 5 + [HBM, ANY],
        out_specs=[HBM, VMEM],
        aliases={5: 0, 6: 1},
        **costs,
    )(*scattered, mine, near0, leaf, product, own)
    return call(
        final_kernel,
        "final",
        [whole],
        [VMEM] * 6 + [HBM],
        flops=LEAF * RANK * NCOL,
        moved=4 * MIB,
        scratch=[pltpu.VMEM((LEAF, HALF), BF16), pltpu.SemaphoreType.DMA((7,))],
        out_specs=[HBM],
        aliases={6: 0},
    )(*scattered, other, near0, leaf, own, product)[0]


def solution(mesh):
    in_specs = (
        P(("gx", "gy"), None),
        P("gx", "gy", None),
        P(("gx", "gy"), None),
        P(("gx", "gy"), None),
        P(("gx", "gy"), None),
        P("gx", "gy", None, None, None),
        P("gx", "gy", None, None, None),
        P(),
    )
    out_specs = P(("gx", "gy"), None)
    return jax.shard_map(local, mesh=mesh, in_specs=in_specs, out_specs=out_specs, check_vma=False)
```

```python
import functools

import jax
import jax.numpy as jnp
from jax import lax
from jax.experimental import pallas as pl
from jax.experimental.pallas import tpu as pltpu
from jax.sharding import PartitionSpec as P

AXES = ("gx", "gy")
F32 = jnp.float32
BF16 = jnp.bfloat16
LEAF = 2048
RANK = 256
NCOL = 768
HALF = NCOL // 2
QUARTER = NCOL // 4
EARLY = 2
VMEM = pl.BlockSpec(memory_space=pltpu.VMEM)
HBM = pl.BlockSpec(memory_space=pltpu.HBM)
ANY = pl.BlockSpec(memory_space=pl.ANY)
MIB = 1 << 20


def permute(array, dx=0, dy=0):
    pairs = [(gx * 8 + gy, (gx ^ dx) * 8 + (gy ^ dy)) for gx in range(16) for gy in range(8)]
    return lax.ppermute(array, AXES, pairs)


def nn(a, b):
    return jnp.dot(a, b, preferred_element_type=F32)


def nt(a, b):
    return lax.dot_general(a, b, (((1,), (1,)), ((), ())), preferred_element_type=F32)


def add(a, b):
    return (a[...].astype(F32) + b[...].astype(F32)).astype(BF16)


def core_index():
    return lax.rem(lax.axis_index("gy"), 2)


def half_columns(own):
    core = core_index()
    return pl.ds(pl.multiple_of((core if own else 1 - core) * HALF, HALF), HALF)


def part_index():
    x = lax.rem(lax.axis_index("gx"), 4)
    return jnp.where((x == 1) | (x == 2), 1, 0)


def early_index():
    gx, gy = lax.axis_index("gx"), lax.axis_index("gy")
    return lax.rem(gx, 4) + gx // 4 + gy // 2 <= EARLY


def call(kernel, name, outs, in_specs, flops=0, moved=0, scratch=(), limit=16, aliases=None, out_specs=None):
    return pl.pallas_call(
        kernel,
        out_shape=[jax.ShapeDtypeStruct(*o) for o in outs],
        in_specs=in_specs,
        out_specs=[VMEM] * len(outs) if out_specs is None else out_specs,
        scratch_shapes=list(scratch),
        input_output_aliases=aliases or {},
        compiler_params=pltpu.CompilerParams(vmem_limit_bytes=limit * MIB),
        cost_estimate=pl.CostEstimate(flops=flops, bytes_accessed=moved, transcendentals=0),
        name=name,
    )


def picks(order_row, base, rows):
    it = lax.broadcasted_iota(jnp.int32, (rows, LEAF), 0)
    return jnp.where(it == (order_row - base), 1.0, 0.0).astype(BF16)


def front_kernel(
    order_hbm, basis_hbm, x_hbm, leaf_hbm, coarse_hbm, basis_out_hbm, top,
    send, c_both, x, order, turned, rows, leaf, coarse, basis_out,
    basis, sems,
):
    pairs = [(order_hbm, order), (basis_hbm, basis), (x_hbm, x), (leaf_hbm, leaf), (coarse_hbm, coarse)]
    pairs.append((basis_out_hbm, basis_out))
    y = lax.axis_index("gx") // 4
    z = lax.axis_index("gy") // 4
    flip = jnp.where(lax.rem(y, 2) == 0, y + 1, y - 1)
    for d, there in enumerate((y, flip, 3 - y, 3 - flip)):
        r = pl.multiple_of((there * 2 + z) * RANK, RANK)
        s = pl.multiple_of(y * 2 * RANK, 2 * RANK)
        pairs.append((top.at[pl.ds(r, RANK), pl.ds(s, 2 * RANK)], rows.at[d]))
    fetches = [pltpu.make_async_copy(here, there, sems.at[i]) for i, (here, there) in enumerate(pairs)]
    for fetch in fetches:
        fetch.start()
    fetches[0].wait()
    fetches[1].wait()
    flat = basis[...].T
    for j in range(LEAF // 512):
        turned[:, j * 512 : (j + 1) * 512] = nt(flat, picks(order[...], j * 512, 512)).astype(BF16)
    fetches[2].wait()
    fetches[3].wait()
    cols = half_columns(False)
    c = nn(turned[...], x[:, cols]).astype(BF16).T
    c_both[cols] = c
    send[...] = nn(c, leaf[0]).astype(BF16)
    for fetch in fetches[4:]:
        fetch.wait()


def own_coef_kernel(turned, x, leaf, _c_both, _after, keep, c_both, c_own):
    cols = half_columns(True)
    c = nn(turned[...], x[:, cols]).astype(BF16).T
    c_both[cols] = c
    keep[...] = nn(c, leaf[0]).astype(BF16)
    c_own[...] = c_both[:NCOL]


def pair_kernel(keep, recv, _after, send2, keep2, total):
    total[...] = add(keep, recv)
    part = part_index()
    keep2[...] = total[pl.ds(pl.multiple_of(part * QUARTER, QUARTER), QUARTER), :]
    send2[...] = total[pl.ds(pl.multiple_of((1 - part) * QUARTER, QUARTER), QUARTER), :]


def fill_kernel(recv, _c_both, _after, c_both):
    c_both[NCOL:] = recv[...]


def coarse_kernel(keep, recv, couple, _after, coef1, lift1):
    c = add(keep, recv)
    coef1[...] = c
    lift1[...] = nn(c, couple[0]).astype(BF16)


def sum_kernel(mine, recv, _after, total):
    total[...] = add(mine, recv)


def both_tops(own, other, keep_own):
    low = lax.axis_index("gy") < 4
    b = other[...]
    a = own[...] if keep_own else jnp.zeros_like(b)
    return jnp.concatenate([jnp.where(low, a, b), jnp.where(low, b, a)], axis=1)


def top_send_kernel(own, other, rows, _after, send):
    both = both_tops(own, other, True)
    send[:QUARTER] = nt(both, rows[2]).astype(BF16)
    send[QUARTER:] = nt(both, rows[3]).astype(BF16)


def top_stay_kernel(own, other, rows, _after, stay0, stay1):
    stay0[...] = nt(both_tops(own, other, False), rows[0])
    stay1[...] = nt(both_tops(own, other, True), rows[1])


def half_kernel(stay1, recv, _after, send):
    send[...] = (stay1[...] + recv[QUARTER:].astype(F32)).astype(BF16)


def near1_kernel(side_x, sides, couple, _after, near1):
    near1[...] = (
        nt(side_x[...], couple[1]) + nt(sides[:QUARTER], couple[2]) + nt(sides[QUARTER:], couple[3])
    )


def near0_kernel(sides, recv, couple, _after, near0):
    near0[...] = nt(couple[1], sides[:NCOL]) + nt(couple[2], recv[...]) + nt(couple[3], sides[NCOL:])


def down1_kernel(stay0, first, second, near1, couple, _after, down1):
    d2 = (stay0[...] + first[:QUARTER].astype(F32) + second[...].astype(F32)).astype(BF16)
    down1[...] = (near1[...] + nt(d2, couple[0])).astype(BF16)


def gather_kernel(blocks, first, order, x, _after, *refs):
    out = refs[first]
    for start, size in blocks:
        parts = []
        for s in range(start, start + size, 128):
            column = jnp.broadcast_to(order[:, s : s + 128].astype(F32), (128, 128)).T
            lane = lax.broadcasted_iota(jnp.int32, (128, 128), 1).astype(F32)
            parts.append(
                jnp.concatenate(
                    [jnp.where(column == lane + 128.0 * j, 1.0, 0.0).astype(BF16) for j in range(LEAF // 128)], axis=1
                )
            )
        out[start : start + size] = nn(jnp.concatenate(parts, axis=0), x[...]).astype(BF16)


def dense_kernel(blocks, first, dense, ordered, _after, *refs):
    out = refs[first]
    for start, size in blocks:
        out[start : start + size] = nn(dense[start : start + size], ordered[...]).astype(BF16)


def early_kernel(order, basis, _after, turned):
    @pl.when(early_index())
    def _():
        for start in range(0, LEAF, 512):
            turned[start : start + 512] = nn(picks(order[...], start, 512), basis[...]).astype(BF16)


def scatter_kernel(early_blocks, blocks, first, order, result, basis, _after, *refs):
    out, turned = refs[first : first + 2]
    early = early_index()

    @pl.when(early)
    def _():
        for start, size in early_blocks:
            out[start : start + size] = nn(picks(order[...], start, size), result[...]).astype(BF16)

    @pl.when(jnp.logical_not(early))
    def _():
        for start, size in blocks:
            hot = picks(order[...], start, size)
            out[start : start + size] = nn(hot, result[...]).astype(BF16)
            turned[start : start + size] = nn(hot, basis[...]).astype(BF16)


def both_kernel(coef1, side_x, _after, both):
    both[:QUARTER] = coef1[...]
    both[QUARTER:] = side_x[...]


def join_kernel(own, side, _after, joined):
    part = part_index()
    joined[pl.ds(pl.multiple_of(part * QUARTER, QUARTER), QUARTER), :] = own[...]
    joined[pl.ds(pl.multiple_of((1 - part) * QUARTER, QUARTER), QUARTER), :] = side[...]


def leaf_half(base, turned, down1, near0, couple, cols, out, after_block):
    down0 = (near0[:, cols] + nt(couple[0], down1[...])).astype(BF16)
    for start, size in ((0, 512), (512, 512), (1024, 512), (1536, 256), (1792, 128), (1920, 128)):
        rows = pl.ds(start, size)
        out[rows] = (base[rows, cols].astype(F32) + nn(turned[rows], down0)).astype(BF16)
        after_block(rows)


def own_half_kernel(which, base, turned, down1, near0, couple, *refs):
    out_hbm, out, sems = refs[-3 - (which == 1)], refs[-2 - (which == 1)], refs[-1]

    @pl.when(core_index() == which)
    def _():
        cols = half_columns(True)
        copies = []

        def write(rows):
            if rows.start < LEAF // 2:
                copies.append(pltpu.make_async_copy(out.at[rows], out_hbm.at[rows, cols], sems.at[len(copies)]))
                copies[-1].start()

        leaf_half(base, turned, down1, near0, couple, cols, out, write)
        for copy in copies:
            copy.wait()


def final_kernel(base, turned, down1, near0, couple, own, _product, out_hbm, out, sems):
    lower = pl.ds(LEAF // 2, LEAF // 2)
    copies = [pltpu.make_async_copy(own.at[lower], out_hbm.at[lower, half_columns(True)], sems.at[0])]
    copies[0].start()
    cols = half_columns(False)

    def write(rows):
        copies.append(pltpu.make_async_copy(out.at[rows], out_hbm.at[rows, cols], sems.at[len(copies)]))
        copies[-1].start()

    leaf_half(base, turned, down1, near0, couple, cols, out, write)
    for copy in copies:
        copy.wait()


def leaf_part(kernel, name, blocks, operands, previous, widths, after, carry=()):
    outs = [((LEAF, width), BF16) for width in widths]
    kept = list(previous) + list(carry)
    count = len(operands) + 1
    skip = len(outs) - len(previous)
    got = call(
        functools.partial(kernel, blocks, len(kept)),
        name,
        outs + [(c.shape, c.dtype) for c in carry],
        [VMEM] * len(operands) + [ANY] + [VMEM] * len(previous) + [ANY] * len(carry),
        flops=2 * sum(size for _, size in blocks) * LEAF * sum(widths),
        moved=4 * MIB,
        aliases={count + i: skip + i for i in range(len(kept))},
        out_specs=[VMEM] * len(outs) + [ANY] * len(carry),
    )(*operands, after, *kept)
    return (got[: len(outs)], *got[len(outs) :])


def local(right_block, point_order, leaf_dense, basis_in, basis_out, leaf_couple, coarse_couple, top_coupling):
    couple = ((4, RANK, RANK), BF16)
    quarter = ((QUARTER, RANK), BF16)
    quarter_f32 = ((QUARTER, RANK), F32)
    half = ((HALF, RANK), BF16)
    small = 2 * QUARTER * RANK * RANK
    widths = [NCOL, RANK]
    gather = functools.partial(leaf_part, gather_kernel, "gather")
    dense = functools.partial(leaf_part, dense_kernel, "dense")

    def scatter(early_blocks, blocks, *rest):
        return leaf_part(functools.partial(scatter_kernel, early_blocks), "scatter", blocks, *rest)


    inputs = (
        point_order.reshape(1, LEAF),
        basis_in,
        right_block,
        leaf_couple.reshape(4, RANK, RANK),
        coarse_couple.reshape(4, RANK, RANK),
        basis_out,
        top_coupling,
    )
    both_coefs = ((2 * NCOL, RANK), BF16)
    send, c_both, x, order, turned_basis, rows, leaf, coarse, basis = call(
        front_kernel,
        "front",
        [
            half,
            both_coefs,
            ((LEAF, NCOL), BF16),
            ((1, LEAF), jnp.int32),
            ((RANK, LEAF), BF16),
            ((4, RANK, 2 * RANK), BF16),
            couple,
            couple,
            ((LEAF, RANK), BF16),
        ],
        [HBM] * 7,
        flops=2 * LEAF * LEAF * RANK + LEAF * RANK * NCOL,
        moved=7 * MIB,
        scratch=[pltpu.VMEM((LEAF, RANK), BF16), pltpu.SemaphoreType.DMA((10,))],
    )(*(pltpu.with_memory_space_constraint(a, pltpu.HBM) for a in inputs))
    recv = permute(send, dy=1)
    keep, c_both, c_own = call(
        own_coef_kernel,
        "own_coef",
        [half, both_coefs, ((NCOL, RANK), BF16)],
        [VMEM] * 4 + [ANY],
        flops=LEAF * RANK * NCOL,
        moved=2 * MIB,
        aliases={3: 1},
    )(turned_basis, x, leaf, c_both, send)
    c_core = permute(c_own, dy=1)

    turned = call(early_kernel, "early", [((LEAF, RANK), BF16)], [VMEM, VMEM, ANY], moved=2 * MIB)(
        order, basis, c_own
    )

    send2, keep2 = call(
        pair_kernel, "pair", [quarter, quarter], [VMEM, VMEM, ANY], scratch=[pltpu.VMEM((HALF, RANK), BF16)]
    )(keep, recv, turned[0])
    recv2 = permute(send2, dx=1)
    (ordered,) = gather([(0, 640), (640, 512)], [order, x], [], [NCOL], send2)

    coef1, lift1 = call(coarse_kernel, "coarse", [quarter, quarter], [VMEM, VMEM, VMEM, ANY], flops=small)(
        keep2, recv2, coarse, ordered[0]
    )
    recv3 = permute(lift1, dx=3)
    (ordered,) = gather([(1152, 512), (1664, 384)], [order, x], ordered, [NCOL], lift1)
    c_both = call(fill_kernel, "fill", [both_coefs], [VMEM, VMEM, ANY], aliases={1: 0})(
        c_core, c_both, ordered[0]
    )[0]
    sides = permute(c_both, dx=1)

    pair = call(sum_kernel, "sum_x", [quarter], [VMEM, VMEM, ANY])(lift1, recv3, c_both)[0]
    recv4 = permute(pair, dy=2)
    result, coef1 = dense([(0, 576)], [leaf_dense, ordered[0]], [], [NCOL], pair, [coef1])
    coarse_x = permute(coef1, dx=3)

    coef2 = call(sum_kernel, "sum_z", [quarter], [VMEM, VMEM, ANY])(pair, recv4, result[0])[0]
    recv5 = permute(coef2, dy=6)
    (result,) = dense([(576, 640)], [leaf_dense, ordered[0]], result, [NCOL], coef2)
    both = call(both_kernel, "both", [half], [VMEM, VMEM, ANY])(coef1, coarse_x, result[0])[0]
    coarse_yz = permute(both, dy=2)

    send6 = call(top_send_kernel, "top_send", [half], [VMEM, VMEM, VMEM, ANY], flops=4 * small)(
        coef2, recv5, rows, both
    )[0]
    recv6 = permute(send6, dx=12)
    stay0, stay1 = call(
        top_stay_kernel, "top_stay", [quarter_f32, quarter_f32], [VMEM, VMEM, VMEM, ANY], flops=4 * small
    )(coef2, recv5, rows, send6)
    (result,) = dense([(1216, 416), (1632, 416)], [leaf_dense, ordered[0]], result, [NCOL], stay0)
    (scattered,) = scatter([(0, 256)], [(0, 512)], [order, result[0], basis], turned, widths, stay0)

    send7 = call(half_kernel, "half", [quarter], [VMEM, VMEM, ANY])(stay1, recv6, scattered[0])[0]
    recv7 = permute(send7, dx=4)
    near1 = call(near1_kernel, "near1", [quarter_f32], [VMEM, VMEM, VMEM, ANY], flops=3 * small)(
        coarse_x, coarse_yz, coarse, send7
    )[0]
    (scattered,) = scatter([(256, 512), (768, 512)], [(512, 768)], [order, result[0], basis], scattered, widths, near1)

    down1 = call(down1_kernel, "down1", [quarter], [VMEM] * 5 + [ANY], flops=small)(
        stay0, recv6, recv7, near1, coarse, scattered[0]
    )[0]
    side = permute(down1, dx=1)
    near0 = call(near0_kernel, "near0", [((RANK, NCOL), F32)], [VMEM] * 3 + [ANY], flops=12 * small)(
        sides, c_core, leaf, down1
    )[0]
    (scattered,) = scatter([(1280, 768)], [(1280, 768)], [order, result[0], basis], scattered, widths, near0)

    mine = call(join_kernel, "join", [half], [VMEM, VMEM, ANY])(down1, side, scattered[0])[0]
    whole = ((LEAF, NCOL), BF16)
    halves = [whole, ((LEAF, HALF), BF16)]
    costs = dict(flops=LEAF * RANK * NCOL, moved=2 * MIB, scratch=[pltpu.SemaphoreType.DMA((2,))])
    product, own, mine = call(
        functools.partial(own_half_kernel, 1),
        "own_half_1",
        halves + [half],
        [VMEM] * 5,
        out_specs=[HBM, VMEM, VMEM],
        aliases={2: 2},
        **costs,
    )(*scattered, mine, near0, leaf)
    other = permute(mine, dy=1)
    product, own = call(
        functools.partial(own_half_kernel, 0),
        "own_half_0",
        halves,
        [VMEM] * 5 + [HBM, ANY],
        out_specs=[HBM, VMEM],
        aliases={5: 0, 6: 1},
        **costs,
    )(*scattered, mine, near0, leaf, product, own)
    return call(
        final_kernel,
        "final",
        [whole],
        [VMEM] * 6 + [HBM],
        flops=LEAF * RANK * NCOL,
        moved=4 * MIB,
        scratch=[pltpu.VMEM((LEAF, HALF), BF16), pltpu.SemaphoreType.DMA((7,))],
        out_specs=[HBM],
        aliases={6: 0},
    )(*scattered, other, near0, leaf, own, product)[0]


def solution(mesh):
    in_specs = (
        P(("gx", "gy"), None),
        P("gx", "gy", None),
        P(("gx", "gy"), None),
        P(("gx", "gy"), None),
        P(("gx", "gy"), None),
        P("gx", "gy", None, None, None),
        P("gx", "gy", None, None, None),
        P(),
    )
    out_specs = P(("gx", "gy"), None)
    return jax.shard_map(local, mesh=mesh, in_specs=in_specs, out_specs=out_specs, check_vma=False)
```

```python
import functools

import jax
import jax.numpy as jnp
from jax import lax
from jax.experimental import pallas as pl
from jax.experimental.pallas import tpu as pltpu
from jax.sharding import PartitionSpec as P

AXES = ("gx", "gy")
F32 = jnp.float32
BF16 = jnp.bfloat16
LEAF = 2048
RANK = 256
NCOL = 768
HALF = NCOL // 2
QUARTER = NCOL // 4
EARLY = 2
VMEM = pl.BlockSpec(memory_space=pltpu.VMEM)
HBM = pl.BlockSpec(memory_space=pltpu.HBM)
ANY = pl.BlockSpec(memory_space=pl.ANY)
MIB = 1 << 20


def permute(array, dx=0, dy=0):
    pairs = [(gx * 8 + gy, (gx ^ dx) * 8 + (gy ^ dy)) for gx in range(16) for gy in range(8)]
    return lax.ppermute(array, AXES, pairs)


def nn(a, b):
    return jnp.dot(a, b, preferred_element_type=F32)


def nt(a, b):
    return lax.dot_general(a, b, (((1,), (1,)), ((), ())), preferred_element_type=F32)


def add(a, b):
    return (a[...].astype(F32) + b[...].astype(F32)).astype(BF16)


def core_index():
    return lax.rem(lax.axis_index("gy"), 2)


def half_columns(own):
    core = core_index()
    return pl.ds(pl.multiple_of((core if own else 1 - core) * HALF, HALF), HALF)


def part_index():
    x = lax.rem(lax.axis_index("gx"), 4)
    return jnp.where((x == 1) | (x == 2), 1, 0)


def early_index():
    gx, gy = lax.axis_index("gx"), lax.axis_index("gy")
    return lax.rem(gx, 4) + gx // 4 + gy // 2 <= EARLY


def call(kernel, name, outs, in_specs, flops=0, moved=0, scratch=(), limit=16, aliases=None, out_specs=None):
    return pl.pallas_call(
        kernel,
        out_shape=[jax.ShapeDtypeStruct(*o) for o in outs],
        in_specs=in_specs,
        out_specs=[VMEM] * len(outs) if out_specs is None else out_specs,
        scratch_shapes=list(scratch),
        input_output_aliases=aliases or {},
        compiler_params=pltpu.CompilerParams(vmem_limit_bytes=limit * MIB),
        cost_estimate=pl.CostEstimate(flops=flops, bytes_accessed=moved, transcendentals=0),
        name=name,
    )


def picks(order_row, base, rows):
    it = lax.broadcasted_iota(jnp.int32, (rows, LEAF), 0)
    return jnp.where(it == (order_row - base), 1.0, 0.0).astype(BF16)


def front_kernel(
    order_hbm, basis_hbm, x_hbm, leaf_hbm, coarse_hbm, basis_out_hbm, top,
    send, c_both, x, order, turned, rows, leaf, coarse, basis_out,
    basis, sems,
):
    pairs = [(order_hbm, order), (basis_hbm, basis), (x_hbm, x), (leaf_hbm, leaf), (coarse_hbm, coarse)]
    pairs.append((basis_out_hbm, basis_out))
    y = lax.axis_index("gx") // 4
    z = lax.axis_index("gy") // 4
    flip = jnp.where(lax.rem(y, 2) == 0, y + 1, y - 1)
    for d, there in enumerate((y, flip, 3 - y, 3 - flip)):
        r = pl.multiple_of((there * 2 + z) * RANK, RANK)
        s = pl.multiple_of(y * 2 * RANK, 2 * RANK)
        pairs.append((top.at[pl.ds(r, RANK), pl.ds(s, 2 * RANK)], rows.at[d]))
    fetches = [pltpu.make_async_copy(here, there, sems.at[i]) for i, (here, there) in enumerate(pairs)]
    for fetch in fetches:
        fetch.start()
    fetches[0].wait()
    fetches[1].wait()
    flat = basis[...].T
    for j in range(LEAF // 512):
        turned[:, j * 512 : (j + 1) * 512] = nt(flat, picks(order[...], j * 512, 512)).astype(BF16)
    fetches[2].wait()
    fetches[3].wait()
    cols = half_columns(False)
    c = nn(turned[...], x[:, cols]).astype(BF16).T
    c_both[cols] = c
    send[...] = nn(c, leaf[0]).astype(BF16)
    for fetch in fetches[4:]:
        fetch.wait()


def own_coef_kernel(turned, x, leaf, _c_both, _after, keep, c_both, c_own):
    cols = half_columns(True)
    c = nn(turned[...], x[:, cols]).astype(BF16).T
    c_both[cols] = c
    keep[...] = nn(c, leaf[0]).astype(BF16)
    c_own[...] = c_both[:NCOL]


def pair_kernel(keep, recv, _after, send2, keep2, total):
    total[...] = add(keep, recv)
    part = part_index()
    keep2[...] = total[pl.ds(pl.multiple_of(part * QUARTER, QUARTER), QUARTER), :]
    send2[...] = total[pl.ds(pl.multiple_of((1 - part) * QUARTER, QUARTER), QUARTER), :]


def fill_kernel(recv, _c_both, _after, c_both):
    c_both[NCOL:] = recv[...]


def coarse_kernel(keep, recv, couple, _after, coef1, lift1):
    c = add(keep, recv)
    coef1[...] = c
    lift1[...] = nn(c, couple[0]).astype(BF16)


def sum_kernel(mine, recv, _after, total):
    total[...] = add(mine, recv)


def both_tops(own, other, keep_own):
    low = lax.axis_index("gy") < 4
    b = other[...]
    a = own[...] if keep_own else jnp.zeros_like(b)
    return jnp.concatenate([jnp.where(low, a, b), jnp.where(low, b, a)], axis=1)


def top_send_kernel(own, other, rows, _after, send):
    both = both_tops(own, other, True)
    send[:QUARTER] = nt(both, rows[2]).astype(BF16)
    send[QUARTER:] = nt(both, rows[3]).astype(BF16)


def top_stay_kernel(own, other, rows, _after, stay0, stay1):
    stay0[...] = nt(both_tops(own, other, False), rows[0])
    stay1[...] = nt(both_tops(own, other, True), rows[1])


def half_kernel(stay1, recv, _after, send):
    send[...] = (stay1[...] + recv[QUARTER:].astype(F32)).astype(BF16)


def near1_kernel(side_x, sides, couple, _after, near1):
    near1[...] = (
        nt(side_x[...], couple[1]) + nt(sides[:QUARTER], couple[2]) + nt(sides[QUARTER:], couple[3])
    )


def near0_kernel(sides, recv, couple, _after, near0):
    near0[...] = nt(couple[1], sides[:NCOL]) + nt(couple[2], recv[...]) + nt(couple[3], sides[NCOL:])


def down1_kernel(stay0, first, second, near1, couple, _after, down1):
    d2 = (stay0[...] + first[:QUARTER].astype(F32) + second[...].astype(F32)).astype(BF16)
    down1[...] = (near1[...] + nt(d2, couple[0])).astype(BF16)


def gather_kernel(blocks, first, order, x, _after, *refs):
    out = refs[first]
    for start, size in blocks:
        parts = []
        for s in range(start, start + size, 128):
            column = jnp.broadcast_to(order[:, s : s + 128].astype(F32), (128, 128)).T
            lane = lax.broadcasted_iota(jnp.int32, (128, 128), 1).astype(F32)
            parts.append(
                jnp.concatenate(
                    [jnp.where(column == lane + 128.0 * j, 1.0, 0.0).astype(BF16) for j in range(LEAF // 128)], axis=1
                )
            )
        out[start : start + size] = nn(jnp.concatenate(parts, axis=0), x[...]).astype(BF16)


def dense_kernel(blocks, first, dense, ordered, _after, *refs):
    out = refs[first]
    for start, size in blocks:
        out[start : start + size] = nn(dense[start : start + size], ordered[...]).astype(BF16)


def early_kernel(order, basis, _after, turned):
    @pl.when(early_index())
    def _():
        for start in range(0, LEAF, 512):
            turned[start : start + 512] = nn(picks(order[...], start, 512), basis[...]).astype(BF16)


def scatter_kernel(early_blocks, blocks, first, order, result, basis, _after, *refs):
    out, turned = refs[first : first + 2]
    early = early_index()

    @pl.when(early)
    def _():
        for start, size in early_blocks:
            out[start : start + size] = nn(picks(order[...], start, size), result[...]).astype(BF16)

    @pl.when(jnp.logical_not(early))
    def _():
        for start, size in blocks:
            hot = picks(order[...], start, size)
            out[start : start + size] = nn(hot, result[...]).astype(BF16)
            turned[start : start + size] = nn(hot, basis[...]).astype(BF16)


def both_kernel(coef1, side_x, _after, both):
    both[:QUARTER] = coef1[...]
    both[QUARTER:] = side_x[...]


def join_kernel(own, side, _after, joined):
    part = part_index()
    joined[pl.ds(pl.multiple_of(part * QUARTER, QUARTER), QUARTER), :] = own[...]
    joined[pl.ds(pl.multiple_of((1 - part) * QUARTER, QUARTER), QUARTER), :] = side[...]


def leaf_half(base, turned, down1, near0, couple, cols, out, after_block):
    down0 = (near0[:, cols] + nt(couple[0], down1[...])).astype(BF16)
    for start, size in ((0, 512), (512, 512), (1024, 512), (1536, 256), (1792, 128), (1920, 128)):
        rows = pl.ds(start, size)
        out[rows] = (base[rows, cols].astype(F32) + nn(turned[rows], down0)).astype(BF16)
        after_block(rows)


def own_half_kernel(which, base, turned, down1, near0, couple, *refs):
    out_hbm, out = refs[:2] if which else refs[2:4]
    sems = refs[-1]

    @pl.when(core_index() == which)
    def _():
        cols = half_columns(True)
        copies = []

        def write(rows):
            if rows.start < LEAF // 2:
                copies.append(pltpu.make_async_copy(out.at[rows], out_hbm.at[rows, cols], sems.at[len(copies)]))
                copies[-1].start()

        leaf_half(base, turned, down1, near0, couple, cols, out, write)
        if which:
            ready, mixed = refs[3:5]
            rest = half_columns(False)
            near = near0[:, rest].astype(BF16)
            for start in range(0, LEAF, 512):
                rows = pl.ds(start, 512)
                ready[rows] = (base[rows, rest].astype(F32) + nn(turned[rows], near)).astype(BF16)
                mixed[rows] = nn(turned[rows], couple[0]).astype(BF16)
        for copy in copies:
            copy.wait()


def final_kernel(base, turned, down1, near0, couple, own, ready, mixed, _product, out_hbm, out, sems):
    lower = pl.ds(LEAF // 2, LEAF // 2)
    cols = half_columns(False)

    def finish(product_rows):
        copies = [pltpu.make_async_copy(own.at[lower], out_hbm.at[lower, half_columns(True)], sems.at[0])]
        copies[0].start()

        def write(rows):
            copies.append(pltpu.make_async_copy(out.at[rows], out_hbm.at[rows, cols], sems.at[len(copies)]))
            copies[-1].start()

        product_rows(write)
        for copy in copies:
            copy.wait()

    def prepared(write):
        down = down1[...].T
        for start, size in ((0, 512), (512, 512), (1024, 512), (1536, 256), (1792, 128), (1920, 128)):
            rows = pl.ds(start, size)
            out[rows] = (ready[rows].astype(F32) + nn(mixed[rows], down)).astype(BF16)
            write(rows)

    core = core_index()
    pl.when(core == 1)(lambda: finish(prepared))
    pl.when(core == 0)(
        lambda: finish(lambda write: leaf_half(base, turned, down1, near0, couple, cols, out, write))
    )


def leaf_part(kernel, name, blocks, operands, previous, widths, after, carry=()):
    outs = [((LEAF, width), BF16) for width in widths]
    kept = list(previous) + list(carry)
    count = len(operands) + 1
    skip = len(outs) - len(previous)
    got = call(
        functools.partial(kernel, blocks, len(kept)),
        name,
        outs + [(c.shape, c.dtype) for c in carry],
        [VMEM] * len(operands) + [ANY] + [VMEM] * len(previous) + [ANY] * len(carry),
        flops=2 * sum(size for _, size in blocks) * LEAF * sum(widths),
        moved=4 * MIB,
        aliases={count + i: skip + i for i in range(len(kept))},
        out_specs=[VMEM] * len(outs) + [ANY] * len(carry),
    )(*operands, after, *kept)
    return (got[: len(outs)], *got[len(outs) :])


def local(right_block, point_order, leaf_dense, basis_in, basis_out, leaf_couple, coarse_couple, top_coupling):
    couple = ((4, RANK, RANK), BF16)
    quarter = ((QUARTER, RANK), BF16)
    quarter_f32 = ((QUARTER, RANK), F32)
    half = ((HALF, RANK), BF16)
    small = 2 * QUARTER * RANK * RANK
    widths = [NCOL, RANK]
    gather = functools.partial(leaf_part, gather_kernel, "gather")
    dense = functools.partial(leaf_part, dense_kernel, "dense")

    def scatter(early_blocks, blocks, *rest):
        return leaf_part(functools.partial(scatter_kernel, early_blocks), "scatter", blocks, *rest)


    inputs = (
        point_order.reshape(1, LEAF),
        basis_in,
        right_block,
        leaf_couple.reshape(4, RANK, RANK),
        coarse_couple.reshape(4, RANK, RANK),
        basis_out,
        top_coupling,
    )
    both_coefs = ((2 * NCOL, RANK), BF16)
    send, c_both, x, order, turned_basis, rows, leaf, coarse, basis = call(
        front_kernel,
        "front",
        [
            half,
            both_coefs,
            ((LEAF, NCOL), BF16),
            ((1, LEAF), jnp.int32),
            ((RANK, LEAF), BF16),
            ((4, RANK, 2 * RANK), BF16),
            couple,
            couple,
            ((LEAF, RANK), BF16),
        ],
        [HBM] * 7,
        flops=2 * LEAF * LEAF * RANK + LEAF * RANK * NCOL,
        moved=7 * MIB,
        scratch=[pltpu.VMEM((LEAF, RANK), BF16), pltpu.SemaphoreType.DMA((10,))],
    )(*(pltpu.with_memory_space_constraint(a, pltpu.HBM) for a in inputs))
    recv = permute(send, dy=1)
    keep, c_both, c_own = call(
        own_coef_kernel,
        "own_coef",
        [half, both_coefs, ((NCOL, RANK), BF16)],
        [VMEM] * 4 + [ANY],
        flops=LEAF * RANK * NCOL,
        moved=2 * MIB,
        aliases={3: 1},
    )(turned_basis, x, leaf, c_both, send)
    c_core = permute(c_own, dy=1)

    turned = call(early_kernel, "early", [((LEAF, RANK), BF16)], [VMEM, VMEM, ANY], moved=2 * MIB)(
        order, basis, c_own
    )

    send2, keep2 = call(
        pair_kernel, "pair", [quarter, quarter], [VMEM, VMEM, ANY], scratch=[pltpu.VMEM((HALF, RANK), BF16)]
    )(keep, recv, turned[0])
    recv2 = permute(send2, dx=1)
    (ordered,) = gather([(0, 640), (640, 512)], [order, x], [], [NCOL], send2)

    coef1, lift1 = call(coarse_kernel, "coarse", [quarter, quarter], [VMEM, VMEM, VMEM, ANY], flops=small)(
        keep2, recv2, coarse, ordered[0]
    )
    recv3 = permute(lift1, dx=3)
    (ordered,) = gather([(1152, 512), (1664, 384)], [order, x], ordered, [NCOL], lift1)
    c_both = call(fill_kernel, "fill", [both_coefs], [VMEM, VMEM, ANY], aliases={1: 0})(
        c_core, c_both, ordered[0]
    )[0]
    sides = permute(c_both, dx=1)

    pair = call(sum_kernel, "sum_x", [quarter], [VMEM, VMEM, ANY])(lift1, recv3, c_both)[0]
    recv4 = permute(pair, dy=2)
    result, coef1 = dense([(0, 576)], [leaf_dense, ordered[0]], [], [NCOL], pair, [coef1])
    coarse_x = permute(coef1, dx=3)

    coef2 = call(sum_kernel, "sum_z", [quarter], [VMEM, VMEM, ANY])(pair, recv4, result[0])[0]
    recv5 = permute(coef2, dy=6)
    (result,) = dense([(576, 640)], [leaf_dense, ordered[0]], result, [NCOL], coef2)
    both = call(both_kernel, "both", [half], [VMEM, VMEM, ANY])(coef1, coarse_x, result[0])[0]
    coarse_yz = permute(both, dy=2)

    send6 = call(top_send_kernel, "top_send", [half], [VMEM, VMEM, VMEM, ANY], flops=4 * small)(
        coef2, recv5, rows, both
    )[0]
    recv6 = permute(send6, dx=12)
    stay0, stay1 = call(
        top_stay_kernel, "top_stay", [quarter_f32, quarter_f32], [VMEM, VMEM, VMEM, ANY], flops=4 * small
    )(coef2, recv5, rows, send6)
    (result,) = dense([(1216, 416), (1632, 416)], [leaf_dense, ordered[0]], result, [NCOL], stay0)
    (scattered,) = scatter([(0, 256)], [(0, 512)], [order, result[0], basis], turned, widths, stay0)

    send7 = call(half_kernel, "half", [quarter], [VMEM, VMEM, ANY])(stay1, recv6, scattered[0])[0]
    recv7 = permute(send7, dx=4)
    near1 = call(near1_kernel, "near1", [quarter_f32], [VMEM, VMEM, VMEM, ANY], flops=3 * small)(
        coarse_x, coarse_yz, coarse, send7
    )[0]
    (scattered,) = scatter([(256, 512), (768, 512)], [(512, 768)], [order, result[0], basis], scattered, widths, near1)

    down1 = call(down1_kernel, "down1", [quarter], [VMEM] * 5 + [ANY], flops=small)(
        stay0, recv6, recv7, near1, coarse, scattered[0]
    )[0]
    side = permute(down1, dx=1)
    near0 = call(near0_kernel, "near0", [((RANK, NCOL), F32)], [VMEM] * 3 + [ANY], flops=12 * small)(
        sides, c_core, leaf, down1
    )[0]
    (scattered,) = scatter([(1280, 768)], [(1280, 768)], [order, result[0], basis], scattered, widths, near0)

    mine = call(join_kernel, "join", [half], [VMEM, VMEM, ANY])(down1, side, scattered[0])[0]
    whole = ((LEAF, NCOL), BF16)
    halves = [whole, ((LEAF, HALF), BF16)]
    costs = dict(flops=LEAF * RANK * NCOL, moved=2 * MIB, scratch=[pltpu.SemaphoreType.DMA((2,))])
    product, own, mine, ready, mixed = call(
        functools.partial(own_half_kernel, 1),
        "own_half_1",
        halves + [half, ((LEAF, HALF), BF16), ((LEAF, RANK), BF16)],
        [VMEM] * 5,
        out_specs=[HBM] + [VMEM] * 4,
        aliases={2: 2},
        **costs,
    )(*scattered, mine, near0, leaf)
    other = permute(mine, dy=1)
    product, own = call(
        functools.partial(own_half_kernel, 0),
        "own_half_0",
        halves,
        [VMEM] * 5 + [HBM, ANY],
        out_specs=[HBM, VMEM],
        aliases={5: 0, 6: 1},
        **costs,
    )(*scattered, mine, near0, leaf, product, own)
    return call(
        final_kernel,
        "final",
        [whole],
        [VMEM] * 8 + [HBM],
        flops=LEAF * RANK * NCOL,
        moved=4 * MIB,
        scratch=[pltpu.VMEM((LEAF, HALF), BF16), pltpu.SemaphoreType.DMA((7,))],
        out_specs=[HBM],
        aliases={8: 0},
    )(*scattered, other, near0, leaf, own, ready, mixed, product)[0]


def solution(mesh):
    in_specs = (
        P(("gx", "gy"), None),
        P("gx", "gy", None),
        P(("gx", "gy"), None),
        P(("gx", "gy"), None),
        P(("gx", "gy"), None),
        P("gx", "gy", None, None, None),
        P("gx", "gy", None, None, None),
        P(),
    )
    out_specs = P(("gx", "gy"), None)
    return jax.shard_map(local, mesh=mesh, in_specs=in_specs, out_specs=out_specs, check_vma=False)
```
